256 devices in a mesh: seq: 64 (over y, z, core), head: 4 (over x).
Axes of the slice: x: 4, y: 4, z: 8, core: 2. Of those that a mesh axis runs over, the one named last changes fastest.
Arguments:
- queries: bfloat16 [32768, 4096], P('seq', 'head'), may hold values from -6 to 6
- keys: bfloat16 [32768, 4096], P('seq', 'head'), may hold values from -0.5 to 0.5
- values: bfloat16 [32768, 4096], P('seq', 'head'), may hold values from -18 to 18
- gate: bfloat16 [32768, 4096], P('seq', 'head'), may hold values from -6 to 6
- gain: float32 [4096], P('head'), may hold values from 0.5 to 2
- dout: bfloat16 [32768, 4096], P('seq', 'head'), may hold values from -6 to 6
Outputs:
- output: bfloat16 [32768, 4096], P('seq', 'head')
- dqueries: bfloat16 [32768, 4096], P('seq', 'head')
- dkeys: bfloat16 [32768, 4096], P('seq', 'head')
- dvalues: bfloat16 [32768, 4096], P('seq', 'head')
- dgate: bfloat16 [32768, 4096], P('seq', 'head')
- dgain: float32 [4096], P('head')
The draws below stay inside these ranges and needn't reach their ends.
All inputs are finite; a program needn't handle non-finite values.
Results may differ from the reference program's by a relative error of at most 0.005.
Values sent between devices are 32-bit elements; how exact they have to be, the bound alone decides.
No kernel may reach another device: no remote copies, remote signals or barrier semaphores. Data moves between devices by JAX's collectives and lax.ppermute only.
A program may use at most 128 MiB of HBM per device.

```python
import math
import jax
import jax.numpy as jnp
from jax import lax

DH = 128
BLOCK = 512
HEADS = 32
TOKENS = 32768


def draw_values(key, part):
    key = jax.random.fold_in(key, 7)
    column = jnp.arange(HEADS * DH)
    level = (column // DH).astype(jnp.float32) / max(HEADS - 1, 1)
    base = jnp.clip(jax.random.normal(key, (TOKENS, HEADS * DH), jnp.float32), -6.0, 6.0)
    factor = jnp.exp(level * jnp.log(3.0))
    return (base * factor[None, :]).astype(jnp.bfloat16)


def block_scale(key, dims, cuts, least, top_value):
    def one(axis_at, parts):
        heights = jax.random.uniform(jax.random.fold_in(jax.random.fold_in(key, 6), axis_at), (parts,), jnp.float32, least / len(cuts), top_value / len(cuts))
        return jnp.repeat(jnp.exp(heights), dims[axis_at] // parts).reshape((-1,) + (1,) * (len(dims) - axis_at - 1))

    loudness = one(*cuts[0])
    for cut in cuts[1:]:
        loudness = loudness * one(*cut)
    return loudness


def gaussian(rng, extent, spread, most, shards=(), kind=jnp.bfloat16):
    values = jax.random.normal(rng, extent, jnp.float32) * spread
    if len(shards) > 0:
        values = block_scale(rng, extent, shards, -0.22, 0.18) * values
    return jnp.clip(values, min=-most, max=most).astype(kind)


def setup_inputs(seed: int = 0) -> dict:
    streams_of = jax.random.split(jax.random.key(seed), 7)
    return {
        "queries": gaussian(streams_of[0], (TOKENS, HEADS * DH), 1.0, 6.0, ((0, 64), (1, 4))),
        "keys": gaussian(streams_of[1], (TOKENS, HEADS * DH), DH ** -0.5, 0.5, ((0, 64), (1, 4))),
        "values": draw_values(jax.random.fold_in(streams_of[6], 71), 0),
        "gate": gaussian(streams_of[3], (TOKENS, HEADS * DH), 1.5, 6.0, ((0, 64), (1, 4))),
        "gain": jnp.clip(jnp.exp(math.log(2.0) - 1.3862944 * jax.random.uniform(streams_of[4], (HEADS * DH,), jnp.float32) ** block_scale(streams_of[4], (HEADS * DH,), ((0, 4),), -0.2, 0.2)), 0.5, 2.0),
        "dout": gaussian(streams_of[5], (TOKENS, HEADS * DH), 1.0, 6.0, ((0, 64), (1, 4))),
    }


epsilon = 1e-06

def block_view(array, count):
    return array.reshape(count, BLOCK, HEADS, DH)

def reference(queries, keys, values, gate, gain, dout):
    highest = lax.Precision.HIGHEST
    count = TOKENS // BLOCK
    causal = jnp.tril(jnp.ones((BLOCK, BLOCK), dtype=bool))
    query_blk = block_view(queries, count)
    key_blk = block_view(keys, count)
    value_blk = block_view(values, count)

    def forward_step(state, pieces):
        query_one, key_one, value_one = pieces
        query_f = query_one.astype(jnp.float32)
        key_f = key_one.astype(jnp.float32)
        value_f = value_one.astype(jnp.float32)
        scores = jnp.einsum('shd,thd->hst', query_f, key_f, precision=highest)
        attend = jnp.where(causal, scores, 0.0).astype(jnp.bfloat16)
        intra = jnp.einsum('hst,the->she', attend.astype(jnp.float32), value_f, precision=highest)
        inter = jnp.einsum('shd,hde->she', query_f, state, precision=highest)
        key_value = jnp.einsum('thd,the->hde', key_f, value_f, precision=highest)
        return (state + key_value, (intra + inter, state))
    start_state = jnp.zeros((HEADS, DH, DH), jnp.float32)
    _, (attn_out, before) = lax.scan(forward_step, start_state, (query_blk, key_blk, value_blk))
    attn_out = attn_out.reshape(TOKENS, HEADS, DH)
    scale_tok = lax.rsqrt(lax.optimization_barrier(jnp.mean(attn_out * attn_out, axis=(1, 2))) + epsilon)[:, None, None]
    gain_hd = gain.reshape(HEADS, DH)
    sig_gate = jax.nn.sigmoid(gate.astype(jnp.float32).reshape(TOKENS, HEADS, DH))
    normed = attn_out * scale_tok * gain_hd
    output = (normed * sig_gate).astype(jnp.bfloat16)
    grad_out = dout.astype(jnp.float32).reshape(TOKENS, HEADS, DH)
    dgate = (grad_out * normed * sig_gate * (1.0 - sig_gate)).astype(jnp.bfloat16)
    grad_normed = grad_out * sig_gate
    dgain = lax.optimization_barrier(jnp.sum(grad_normed * attn_out * scale_tok, axis=0))
    grad_scaled = grad_normed * gain_hd
    mean_prod = lax.optimization_barrier(jnp.mean(grad_scaled * attn_out, axis=(1, 2)))[:, None, None]
    grad_attn = (scale_tok * grad_scaled - attn_out * scale_tok ** 3 * mean_prod).astype(jnp.bfloat16)
    grad_blk = block_view(grad_attn, count)

    def backward_step(state, pieces):
        query_one, key_one, value_one, grad_one, before_one = pieces
        query_f = query_one.astype(jnp.float32)
        key_f = key_one.astype(jnp.float32)
        value_f = value_one.astype(jnp.float32)
        grad_f = grad_one.astype(jnp.float32)
        scores = jnp.einsum('shd,thd->hst', query_f, key_f, precision=highest)
        attend = jnp.where(causal, scores, 0.0).astype(jnp.bfloat16).astype(jnp.float32)
        back_scores = jnp.einsum('she,the->hst', grad_f, value_f, precision=highest)
        back_attend = jnp.where(causal, back_scores, 0.0).astype(jnp.bfloat16).astype(jnp.float32)
        grad_query = jnp.einsum('hst,thd->shd', back_attend, key_f, precision=highest)
        grad_query = grad_query + jnp.einsum('she,hde->shd', grad_f, before_one, precision=highest)
        grad_key = jnp.einsum('hst,shd->thd', back_attend, query_f, precision=highest)
        grad_key = grad_key + jnp.einsum('the,hde->thd', value_f, state, precision=highest)
        grad_value = jnp.einsum('hst,she->the', attend, grad_f, precision=highest)
        grad_value = grad_value + jnp.einsum('thd,hde->the', key_f, state, precision=highest)
        grad_state = jnp.einsum('shd,she->hde', query_f, grad_f, precision=highest)
        return (state + grad_state, (grad_query, grad_key, grad_value))
    _, (grad_query, grad_key, grad_value) = lax.scan(backward_step, start_state, (query_blk, key_blk, value_blk, grad_blk, before), reverse=True)
    flat = (TOKENS, HEADS * DH)
    return (output.reshape(flat), grad_query.reshape(flat).astype(jnp.bfloat16), grad_key.reshape(flat).astype(jnp.bfloat16), grad_value.reshape(flat).astype(jnp.bfloat16), dgate.reshape(flat), dgain.reshape(HEADS * DH))
```

```python
import functools
import jax
import jax.numpy as jnp
from jax import lax
from jax.experimental import pallas as pl
from jax.experimental.pallas import tpu as pltpu
from jax.sharding import PartitionSpec as P

DH = 128
BLOCK = 512
HALF = BLOCK // 2
HEADS_HERE = 8
OWNED = HEADS_HERE // 2
FEATURES = 4096
CHIPS = 32
PIECE = OWNED * DH // CHIPS
EXTRA = 8
EPSILON = 1e-06

F32 = jnp.float32
BF16 = jnp.bfloat16
VMEM_LIMIT = 24 * 1024 * 1024


def dot_nn(a, b):
    return lax.dot_general(a, b, (((1,), (0,)), ((), ())), preferred_element_type=F32)


def dot_nt(a, b):
    return lax.dot_general(a, b, (((1,), (1,)), ((), ())), preferred_element_type=F32)


def dot_tn(a, b):
    return lax.dot_general(a, b, (((0,), (0,)), ((), ())), preferred_element_type=F32)


def split_state(state):
    high = state.astype(BF16)
    return high, (state - high.astype(F32)).astype(BF16)


def times_state(a, state):
    high, low = split_state(state)
    return dot_nn(jnp.concatenate([a, a], axis=1), jnp.concatenate([high, low], axis=0))


def times_state_t(a, state):
    high, low = split_state(state)
    return dot_nt(jnp.concatenate([a, a], axis=1), jnp.concatenate([high, low], axis=1))


def masked(scores, lower):
    row = lax.broadcasted_iota(jnp.int32, scores.shape, 0)
    column = lax.broadcasted_iota(jnp.int32, scores.shape, 1)
    keep = (row >= column) if lower else (row <= column)
    return jnp.where(keep, scores, 0.0).astype(BF16)


def causal_product(a, b, values):
    top = masked(dot_nt(a[:HALF], b[:HALF]), True)
    left = dot_nt(a[HALF:], b[:HALF]).astype(BF16)
    right = masked(dot_nt(a[HALF:], b[HALF:]), True)
    first = dot_nn(top, values[:HALF])
    second = dot_nn(jnp.concatenate([left, right], axis=1), values)
    return first, second


def anticausal_product(a, b, values):
    left = masked(dot_nt(a[:HALF], b[:HALF]), False)
    right = dot_nt(a[:HALF], b[HALF:]).astype(BF16)
    bottom = masked(dot_nt(a[HALF:], b[HALF:]), False)
    first = dot_nn(jnp.concatenate([left, right], axis=1), values)
    second = dot_nn(bottom, values[HALF:])
    return first, second


def params():
    return pltpu.CompilerParams(vmem_limit_bytes=VMEM_LIMIT)


def shape(dims, dtype=F32):
    return jax.ShapeDtypeStruct(dims, dtype)


def head_of(step, core):
    return jnp.where(step < OWNED, OWNED * (1 - core[0]) + step, OWNED * core[0] + step - OWNED)


def column_spec():
    return pl.BlockSpec((BLOCK, DH), lambda i, core: (0, head_of(i, core)))


def theirs_spec(rows):
    return pl.BlockSpec((1, rows, DH), lambda i, core: (jnp.minimum(i, OWNED - 1), 0, 0))


def mine_spec(rows):
    return pl.BlockSpec((1, rows, DH), lambda i, core: (jnp.maximum(i - OWNED, 0), 0, 0))


def state_kernel(core, key, value, theirs, mine):
    step = pl.program_id(0)
    state = dot_tn(key[...], value[...])

    @pl.when(step < OWNED)
    def _():
        theirs[0] = state

    @pl.when(step >= OWNED)
    def _():
        mine[0] = state


def own_states(core, keys, values):
    return pl.pallas_call(
        state_kernel,
        grid_spec=pltpu.PrefetchScalarGridSpec(
            num_scalar_prefetch=1,
            grid=(HEADS_HERE,),
            in_specs=[column_spec(), column_spec()],
            out_specs=[theirs_spec(DH), mine_spec(DH)],
        ),
        out_shape=[shape((OWNED, DH, DH))] * 2,
        compiler_params=params(),
        name="own_states",
    )(core, keys, values)


def intra_kernel(query, key, value, gate, dout, intra, grad_normed):
    first, second = causal_product(query[...], key[...], value[...])
    intra[:HALF] = first
    intra[HALF:] = second
    grad_normed[...] = dout[...].astype(F32) * jax.nn.sigmoid(gate[...].astype(F32))


def plain_column():
    return pl.BlockSpec((BLOCK, DH), lambda i: (0, i))


def intra_part(queries, keys, values, gate, dout):
    wide = (BLOCK, HEADS_HERE * DH)
    return pl.pallas_call(
        intra_kernel,
        grid=(HEADS_HERE,),
        in_specs=[plain_column()] * 5,
        out_specs=[plain_column()] * 2,
        out_shape=[shape(wide), shape(wide)],
        compiler_params=params(),
        name="intra",
    )(queries, keys, values, gate, dout)


def select_state(core, step, own, other):
    return jnp.where(step // OWNED == core[0], own[0, :DH], other[0, :DH])


def attend_kernel(core, query, intra, grad_normed, gain, own, other, attn_out, sums, squares, products):
    step = pl.program_id(0)
    state = select_state(core, step, own, other)
    out = intra[...] + times_state(query[...], state)
    attn_out[...] = out
    square = out * out
    product = out * (grad_normed[...] * gain[...])

    @pl.when(step == 0)
    def _():
        squares[...] = square
        products[...] = product

    @pl.when(step > 0)
    def _():
        squares[...] += square
        products[...] += product

    @pl.when(step == HEADS_HERE - 1)
    def _():
        for which, acc in enumerate((squares, products)):
            for part in range(BLOCK // DH):
                turned = acc[part * DH:(part + 1) * DH, :].T
                place = which * (BLOCK // DH) + part
                sums[place:place + 1, :] = jnp.sum(turned, axis=0, keepdims=True)


def core_column():
    return pl.BlockSpec((BLOCK, DH), lambda i, core: (0, i))


def core_state(rows):
    return pl.BlockSpec((1, rows, DH), lambda i, core: (lax.rem(i, OWNED), 0, 0))


def gain_spec():
    return pl.BlockSpec((1, DH), lambda i, core: (0, i))


def attend(core, queries, intra, grad_normed, gain, own, other):
    return pl.pallas_call(
        attend_kernel,
        grid_spec=pltpu.PrefetchScalarGridSpec(
            num_scalar_prefetch=1,
            grid=(HEADS_HERE,),
            in_specs=[core_column()] * 3 + [gain_spec()] + [core_state(DH)] * 2,
            out_specs=[core_column(), pl.BlockSpec((8, DH), lambda i, core: (0, 0))],
            scratch_shapes=[pltpu.VMEM((BLOCK, DH), F32)] * 2,
        ),
        out_shape=[shape((BLOCK, HEADS_HERE * DH)), shape((8, DH))],
        compiler_params=params(),
        name="attend",
    )(core, queries, intra, grad_normed, gain, own, other)


def grad_kernel(core, sums, query, attn_out, grad_normed, gain, grad, scale, theirs, mine, cubes):
    step = pl.program_id(0)

    @pl.when(step == 0)
    def _():
        for part in range(BLOCK // DH):
            rows = slice(part * DH, (part + 1) * DH)
            mean_square = sums[part:part + 1, :] / FEATURES
            mean_prod = sums[part + 4:part + 5, :] / FEATURES
            one = lax.rsqrt(mean_square + EPSILON)
            scale[rows, :] = jnp.broadcast_to(one, (DH, DH)).T
            cubes[rows, :] = jnp.broadcast_to(one * one * one * mean_prod, (DH, DH)).T

    out = attn_out[...]
    rate = scale[...]
    normed = grad_normed[...]
    here = (rate * (normed * gain[...]) - out * cubes[...]).astype(BF16)
    grad[...] = here
    state = dot_tn(query[...], here)
    gain_row = jnp.sum(normed * out * rate, axis=0, keepdims=True)
    extra = jnp.broadcast_to(gain_row, (EXTRA, DH))

    @pl.when(step < OWNED)
    def _():
        theirs[0, :DH] = state
        theirs[0, DH:] = extra

    @pl.when(step >= OWNED)
    def _():
        mine[0, :DH] = state
        mine[0, DH:] = extra


def token_grads(core, sums, queries, attn_out, grad_normed, gain):
    whole = pl.BlockSpec((8, DH), lambda i, core: (0, 0))
    gain_col = pl.BlockSpec((1, DH), lambda i, core: (0, head_of(i, core)))
    return pl.pallas_call(
        grad_kernel,
        grid_spec=pltpu.PrefetchScalarGridSpec(
            num_scalar_prefetch=1,
            grid=(HEADS_HERE,),
            in_specs=[whole] + [column_spec()] * 3 + [gain_col],
            out_specs=[
                column_spec(),
                pl.BlockSpec((BLOCK, DH), lambda i, core: (0, 0)),
                theirs_spec(DH + EXTRA),
                mine_spec(DH + EXTRA),
            ],
            scratch_shapes=[pltpu.VMEM((BLOCK, DH), F32)],
        ),
        out_shape=[
            shape((BLOCK, HEADS_HERE * DH), BF16),
            shape((BLOCK, DH)),
            shape((OWNED, DH + EXTRA, DH)),
            shape((OWNED, DH + EXTRA, DH)),
        ],
        compiler_params=params(),
        name="token_grads",
    )(core, sums, queries, attn_out, grad_normed, gain)


def local_kernel(core, query, key, value, gate, dout, attn_out, scale, gain, grad, own, other,
                 output, dgate, grad_query, grad_key, grad_value):
    step = pl.program_id(0)
    state = select_state(core, step, own, other)
    sig = jax.nn.sigmoid(gate[...].astype(F32))
    normed = attn_out[...] * scale[...] * gain[...]
    result = normed * sig
    output[...] = result.astype(BF16)
    dgate[...] = (dout[...].astype(F32) * result * (1.0 - sig)).astype(BF16)
    query_here, key_here, value_here, grad_here = query[...], key[...], value[...], grad[...]
    inter = times_state_t(grad_here, state)
    first, second = causal_product(grad_here, value_here, key_here)
    grad_query[:HALF] = (first + inter[:HALF]).astype(BF16)
    grad_query[HALF:] = (second + inter[HALF:]).astype(BF16)
    first, second = anticausal_product(value_here, grad_here, query_here)
    grad_key[:HALF] = first
    grad_key[HALF:] = second
    first, second = anticausal_product(key_here, query_here, grad_here)
    grad_value[:HALF] = first
    grad_value[HALF:] = second


def local_grads(core, queries, keys, values, gate, dout, attn_out, scale, gain, grad, own, other):
    wide = (BLOCK, HEADS_HERE * DH)
    return pl.pallas_call(
        local_kernel,
        grid_spec=pltpu.PrefetchScalarGridSpec(
            num_scalar_prefetch=1,
            grid=(HEADS_HERE,),
            in_specs=[core_column()] * 6
            + [pl.BlockSpec((BLOCK, DH), lambda i, core: (0, 0)), gain_spec(), core_column()]
            + [core_state(DH)] * 2,
            out_specs=[core_column()] * 5,
        ),
        out_shape=[shape(wide, BF16)] * 3 + [shape(wide)] * 2,
        compiler_params=params(),
        name="local_grads",
    )(core, queries, keys, values, gate, dout, attn_out, scale, gain, grad, own, other)


def last_kernel(core, key, value, part_key, part_value, own, other, grad_key, grad_value, dgain):
    step = pl.program_id(0)
    here = step // OWNED == core[0]
    state = jnp.where(here, own[0, :DH], other[0, :DH])
    dgain[pl.ds(step, 1), :] = jnp.where(here, own[0, DH:DH + 1], other[0, DH:DH + 1])
    grad_key[...] = (part_key[...] + times_state_t(value[...], state)).astype(BF16)
    grad_value[...] = (part_value[...] + times_state(key[...], state)).astype(BF16)


def last_grads(core, keys, values, part_key, part_value, own, other):
    wide = (BLOCK, HEADS_HERE * DH)
    return pl.pallas_call(
        last_kernel,
        grid_spec=pltpu.PrefetchScalarGridSpec(
            num_scalar_prefetch=1,
            grid=(HEADS_HERE,),
            in_specs=[core_column()] * 4 + [core_state(DH + EXTRA)] * 2,
            out_specs=[core_column()] * 2
            + [pl.BlockSpec((HEADS_HERE, DH), lambda i, core: (0, 0))],
        ),
        out_shape=[shape(wide, BF16)] * 2 + [shape((HEADS_HERE, DH))],
        compiler_params=params(),
        name="last_grads",
    )(core, keys, values, part_key, part_value, own, other)


def pack_kernel(mine, received, pieces):
    extra = pieces.shape[1] - PIECE
    for head in range(OWNED):
        for part in range(DH // PIECE):
            rows = slice(part * PIECE, (part + 1) * PIECE)
            place = head * (DH // PIECE) + part
            pieces[place, :PIECE] = mine[head, rows] + received[head, rows]
            if extra:
                pieces[place, PIECE:] = mine[head, DH:] + received[head, DH:]


def prefix_kernel(reverse, pieces, sums):
    extra = pieces.shape[1] - PIECE
    total = jnp.zeros((PIECE, DH), F32)
    order = range(CHIPS - 1, -1, -1) if reverse else range(CHIPS)
    for chip in order:
        sums[chip, :PIECE] = total
        total = total + pieces[chip, :PIECE]
    if extra:
        whole = pieces[0, PIECE:]
        for chip in range(1, CHIPS):
            whole = whole + pieces[chip, PIECE:]
        for chip in range(CHIPS):
            sums[chip, PIECE:] = whole


def unpack_kernel(reverse, core, back, mine, received, own, send):
    extra = back.shape[1] - PIECE
    ahead = core[0] == (1 if reverse else 0)
    for head in range(OWNED):
        for part in range(DH // PIECE):
            rows = slice(part * PIECE, (part + 1) * PIECE)
            state = back[head * (DH // PIECE) + part, :PIECE]
            own[head, rows] = state + jnp.where(ahead, 0.0, received[head, rows])
            send[head, rows] = state + jnp.where(ahead, mine[head, rows], 0.0)
        if extra:
            whole = back[head * (DH // PIECE), PIECE:]
            own[head, DH:] = whole
            send[head, DH:] = whole


def vmem():
    return pl.BlockSpec(memory_space=pltpu.VMEM)


def sums_beyond(core, mine, theirs, seq_size, reverse):
    cores = [(i, i ^ 1) for i in range(seq_size)]
    groups = [[2 * i + one for i in range(seq_size // 2)] for one in range(2)]
    extra = mine.shape[1] - DH
    piece = (CHIPS, PIECE + extra, DH)
    received = lax.ppermute(theirs, "seq", cores)
    if extra:
        pieces = pl.pallas_call(
            pack_kernel,
            in_specs=[vmem()] * 2,
            out_specs=vmem(),
            out_shape=shape(piece),
            compiler_params=params(),
            name="pack",
        )(mine, received)
    else:
        pieces = (mine + received).reshape(piece)
    gathered = lax.all_to_all(pieces, "seq", 0, 0, axis_index_groups=groups)
    sums = pl.pallas_call(
        functools.partial(prefix_kernel, reverse),
        in_specs=[vmem()],
        out_specs=vmem(),
        out_shape=shape(piece),
        compiler_params=params(),
        name="prefix",
    )(gathered)
    back = lax.all_to_all(sums, "seq", 0, 0, axis_index_groups=groups)
    own, send = pl.pallas_call(
        functools.partial(unpack_kernel, reverse),
        in_specs=[pl.BlockSpec(memory_space=pltpu.SMEM)] + [vmem()] * 3,
        out_specs=[vmem()] * 2,
        out_shape=[shape(mine.shape)] * 2,
        compiler_params=params(),
        name="unpack",
    )(core, back, mine, received)
    return own, lax.ppermute(send, "seq", cores)


def body(queries, keys, values, gate, gain, dout):
    seq_size = lax.axis_size("seq")
    core = lax.rem(lax.axis_index("seq"), 2).astype(jnp.int32).reshape(1)
    gain_row = gain.reshape(1, HEADS_HERE * DH)
    theirs, mine = own_states(core, keys, values)
    own, other = sums_beyond(core, mine, theirs, seq_size, False)
    intra, grad_normed = intra_part(queries, keys, values, gate, dout)
    attn_out, sums = attend(core, queries, intra, grad_normed, gain_row, own, other)
    sums = lax.psum(sums, "head")
    grad, scale, theirs, mine = token_grads(core, sums, queries, attn_out, grad_normed, gain_row)
    output, dgate, grad_query, part_key, part_value = local_grads(
        core, queries, keys, values, gate, dout, attn_out, scale, gain_row, grad, own, other
    )
    own, other = sums_beyond(core, mine, theirs, seq_size, True)
    grad_key, grad_value, dgain = last_grads(core, keys, values, part_key, part_value, own, other)
    return output, grad_query, grad_key, grad_value, dgate, dgain.reshape(HEADS_HERE * DH)


def solution(mesh):
    wide = P("seq", "head")
    return jax.shard_map(
        body,
        mesh=mesh,
        in_specs=(wide, wide, wide, wide, P("head"), wide),
        out_specs=(wide, wide, wide, wide, wide, P("head")),
        check_vma=False,
    )
```

```python
import functools
import jax
import jax.numpy as jnp
from jax import lax
from jax.experimental import pallas as pl
from jax.experimental.pallas import tpu as pltpu
from jax.sharding import PartitionSpec as P

DH = 128
BLOCK = 512
HALF = BLOCK // 2
HEADS_HERE = 8
OWNED = HEADS_HERE // 2
FEATURES = 4096
CHIPS = 32
PIECE = OWNED * DH // CHIPS
EXTRA = 8
EPSILON = 1e-06

F32 = jnp.float32
BF16 = jnp.bfloat16
MIB = 1024 * 1024


def dot_nn(a, b):
    return lax.dot_general(a, b, (((1,), (0,)), ((), ())), preferred_element_type=F32)


def dot_nt(a, b):
    return lax.dot_general(a, b, (((1,), (1,)), ((), ())), preferred_element_type=F32)


def dot_tn(a, b):
    return lax.dot_general(a, b, (((0,), (0,)), ((), ())), preferred_element_type=F32)


def split_state(state):
    high = state.astype(BF16)
    return high, (state - high.astype(F32)).astype(BF16)


def times_state(a, state):
    high, low = split_state(state)
    return dot_nn(jnp.concatenate([a, a], axis=1), jnp.concatenate([high, low], axis=0))


def times_state_t(a, state):
    high, low = split_state(state)
    return dot_nt(jnp.concatenate([a, a], axis=1), jnp.concatenate([high, low], axis=1))


def masked(scores, lower):
    row = lax.broadcasted_iota(jnp.int32, scores.shape, 0)
    column = lax.broadcasted_iota(jnp.int32, scores.shape, 1)
    keep = (row >= column) if lower else (row <= column)
    return jnp.where(keep, scores, 0.0).astype(BF16)


def causal_product(a, b, values):
    top = masked(dot_nt(a[:HALF], b[:HALF]), True)
    left = dot_nt(a[HALF:], b[:HALF]).astype(BF16)
    right = masked(dot_nt(a[HALF:], b[HALF:]), True)
    first = dot_nn(top, values[:HALF])
    second = dot_nn(jnp.concatenate([left, right], axis=1), values)
    return first, second


def anticausal_product(a, b, values):
    left = masked(dot_nt(a[:HALF], b[:HALF]), False)
    right = dot_nt(a[:HALF], b[HALF:]).astype(BF16)
    bottom = masked(dot_nt(a[HALF:], b[HALF:]), False)
    first = dot_nn(jnp.concatenate([left, right], axis=1), values)
    second = dot_nn(bottom, values[HALF:])
    return first, second


WIDE = HEADS_HERE * DH
HALF_WIDE = OWNED * DH


def shape(dims, dtype=F32):
    return jax.ShapeDtypeStruct(dims, dtype)


def vmem():
    return pl.BlockSpec(memory_space=pltpu.VMEM)


def smem():
    return pl.BlockSpec(memory_space=pltpu.SMEM)


def hbm():
    return pl.BlockSpec(memory_space=pltpu.HBM)


def call(kernel, name, outs, core, *args, ins=None, out_places=None, scratch=(), limit=8):
    ins = [vmem()] * len(args) if ins is None else ins
    out_places = [vmem()] * len(outs) if out_places is None else out_places
    return pl.pallas_call(
        kernel,
        in_specs=[smem()] + ins,
        out_specs=out_places,
        out_shape=outs,
        scratch_shapes=list(scratch),
        compiler_params=pltpu.CompilerParams(vmem_limit_bytes=limit * MIB),
        name=name,
    )(core, *args)


def head_columns(core, owned, index):
    first = OWNED * (core[0] if owned else 1 - core[0])
    return pl.ds(pl.multiple_of((first + index) * DH, DH), DH)


def local_columns(index):
    return slice(index * DH, (index + 1) * DH)


def states_theirs_kernel(core, keys, values, theirs, key_here, value_here, sems):
    copies = []
    for owned in (False, True):
        for index in range(OWNED):
            columns = head_columns(core, owned, index)
            place = len(copies)
            pair = [
                pltpu.make_async_copy(keys.at[:, columns], key_here.at[:, columns], sems.at[0, place]),
                pltpu.make_async_copy(values.at[:, columns], value_here.at[:, columns], sems.at[1, place]),
            ]
            for copy in pair:
                copy.start()
            copies.append(pair)
    for index in range(OWNED):
        for copy in copies[index]:
            copy.wait()
        columns = head_columns(core, False, index)
        theirs[index] = dot_tn(key_here[:, columns], value_here[:, columns])
    for pair in copies[OWNED:]:
        for copy in pair:
            copy.wait()


def states_mine_kernel(core, keys, values, mine):
    for index in range(OWNED):
        columns = head_columns(core, True, index)
        mine[index] = dot_tn(keys[:, columns], values[:, columns])


def intra_kernel(core, queries, keys, values, gate, dout, intra_own, intra_other, normed_own, normed_other):
    for owned, intra, normed in ((True, intra_own, normed_own), (False, intra_other, normed_other)):
        for index in range(OWNED):
            columns, here = head_columns(core, owned, index), local_columns(index)
            first, second = causal_product(queries[:, columns], keys[:, columns], values[:, columns])
            intra[:HALF, here] = first
            intra[HALF:, here] = second
            sig = jax.nn.sigmoid(gate[:, columns].astype(F32))
            normed[:, here] = dout[:, columns].astype(F32) * sig


def intra_part(core, queries, keys, values, gate, dout):
    half = shape((BLOCK, HALF_WIDE))
    return call(intra_kernel, "intra", [half] * 4, core, queries, keys, values, gate, dout)


def attend_half(core, owned, queries, intra, normed, gain, state, attn_out):
    squares = products = None
    for index in range(OWNED):
        columns, here = head_columns(core, owned, index), local_columns(index)
        out = intra[:, here] + times_state(queries[:, columns], state[index, :DH])
        attn_out[:, here] = out
        square = out * out
        product = out * (normed[:, here] * gain[:, columns])
        squares = square if squares is None else squares + square
        products = product if products is None else products + product
    return squares, products


def attend_own_kernel(core, queries, intra, normed, gain, state, attn_out, squares, products):
    squares[...], products[...] = attend_half(core, True, queries, intra, normed, gain, state, attn_out)


def attend_other_kernel(core, queries, intra, normed, gain, state, squares, products, attn_out, sums):
    found = attend_half(core, False, queries, intra, normed, gain, state, attn_out)
    for which, (acc, more) in enumerate(zip((squares, products), found)):
        total = acc[...] + more
        for part in range(BLOCK // DH):
            turned = total[part * DH:(part + 1) * DH, :].T
            place = which * (BLOCK // DH) + part
            sums[place:place + 1, :] = jnp.sum(turned, axis=0, keepdims=True)


def grads_half(core, owned, queries, attn_out, normed, gain, scale, cubes, grad, states):
    for index in range(OWNED):
        columns, here = head_columns(core, owned, index), local_columns(index)
        out, rate, one = attn_out[:, here], scale[...], normed[:, here]
        part = (rate * (one * gain[:, columns]) - out * cubes[...]).astype(BF16)
        grad[:, here] = part
        states[index, :DH] = dot_tn(queries[:, columns], part)
        row = jnp.sum(one * out * rate, axis=0, keepdims=True)
        states[index, DH:] = jnp.broadcast_to(row, (EXTRA, DH))


def grads_theirs_kernel(core, sums, sums_1, sums_2, sums_3, queries, attn_out, normed, gain,
                        grad, scale, cubes, theirs):
    whole = (sums[...] + sums_1[...]) + (sums_2[...] + sums_3[...])
    for part in range(BLOCK // DH):
        rows = slice(part * DH, (part + 1) * DH)
        mean_square = whole[part:part + 1, :] / FEATURES
        mean_prod = whole[part + 4:part + 5, :] / FEATURES
        one = lax.rsqrt(mean_square + EPSILON)
        scale[rows, :] = jnp.broadcast_to(one, (DH, DH)).T
        cubes[rows, :] = jnp.broadcast_to(one * one * one * mean_prod, (DH, DH)).T
    grads_half(core, False, queries, attn_out, normed, gain, scale, cubes, grad, theirs)


def grads_mine_kernel(core, scale, cubes, queries, attn_out, normed, gain, grad, mine):
    grads_half(core, True, queries, attn_out, normed, gain, scale, cubes, grad, mine)


def local_kernel(core, queries, keys, values, gate, out_own, out_other, normed_own, normed_other,
                 scale, gain, grad_own, grad_other, own, other,
                 output, dgate, grad_query, key_own, key_other, value_own, value_other,
                 output_buf, dgate_buf, query_buf, sems):
    halves = (
        (True, out_own, normed_own, grad_own, own, key_own, value_own),
        (False, out_other, normed_other, grad_other, other, key_other, value_other),
    )
    copies = []
    for owned, attn_out, normed, grads, states, part_key, part_value in halves:
        for index in range(OWNED):
            columns, here = head_columns(core, owned, index), local_columns(index)
            place = index if owned else OWNED + index
            sig = jax.nn.sigmoid(gate[:, columns].astype(F32))
            scaled = attn_out[:, here] * scale[...] * gain[:, columns]
            output_buf[place] = (scaled * sig).astype(BF16)
            dgate_buf[place] = (normed[:, here] * scaled * (1.0 - sig)).astype(BF16)
            query, key, value, grad = queries[:, columns], keys[:, columns], values[:, columns], grads[:, here]
            inter = times_state_t(grad, states[index, :DH])
            first, second = causal_product(grad, value, key)
            query_buf[place, :HALF] = (first + inter[:HALF]).astype(BF16)
            query_buf[place, HALF:] = (second + inter[HALF:]).astype(BF16)
            first, second = anticausal_product(value, grad, query)
            part_key[:HALF, here] = first
            part_key[HALF:, here] = second
            first, second = anticausal_product(key, query, grad)
            part_value[:HALF, here] = first
            part_value[HALF:, here] = second
            targets = ((output_buf, output), (dgate_buf, dgate), (query_buf, grad_query))
            for which, (buffer, target) in enumerate(targets):
                copy = pltpu.make_async_copy(buffer.at[place], target.at[:, columns], sems.at[which, place])
                copy.start()
                copies.append(copy)
    for copy in copies:
        copy.wait()


def last_kernel(core, keys, values, key_own, key_other, value_own, value_other, own, other,
                grad_key, grad_value, dgain, key_buf, value_buf, sems):
    copies = []
    halves = ((True, key_own, value_own, own), (False, key_other, value_other, other))
    for owned, part_key, part_value, states in halves:
        for index in range(OWNED):
            columns, here = head_columns(core, owned, index), local_columns(index)
            place = index if owned else OWNED + index
            state = states[index, :DH]
            key_buf[place] = (part_key[:, here] + times_state_t(values[:, columns], state)).astype(BF16)
            value_buf[place] = (part_value[:, here] + times_state(keys[:, columns], state)).astype(BF16)
            pair = [
                pltpu.make_async_copy(key_buf.at[place], grad_key.at[:, columns], sems.at[0, place]),
                pltpu.make_async_copy(value_buf.at[place], grad_value.at[:, columns], sems.at[1, place]),
            ]
            for copy in pair:
                copy.start()
            copies += pair
            row = OWNED * (core[0] if owned else 1 - core[0]) + index
            dgain[pl.ds(row, 1), :] = states[index, DH:DH + 1]
    for copy in copies:
        copy.wait()


def piece_rows(place, rows):
    return slice(place * rows, place * rows + PIECE)


def pack_kernel(rows, core, mine, received, pieces):
    for head in range(OWNED):
        for part in range(DH // PIECE):
            source = slice(part * PIECE, (part + 1) * PIECE)
            place = head * (DH // PIECE) + part
            pieces[piece_rows(place, rows)] = mine[head, source] + received[head, source]
            if rows > PIECE:
                last = place * rows + PIECE
                pieces[last:last + 1] = mine[head, DH:DH + 1] + received[head, DH:DH + 1]


def prefix_kernel(rows, reverse, core, pieces, sums):
    total = jnp.zeros((PIECE, DH), F32)
    order = range(CHIPS - 1, -1, -1) if reverse else range(CHIPS)
    for chip in order:
        sums[piece_rows(chip, rows)] = total
        total = total + pieces[piece_rows(chip, rows)]
    if rows > PIECE:
        places = [slice(chip * rows + PIECE, (chip + 1) * rows) for chip in range(CHIPS)]
        whole = pieces[places[0]]
        for place in places[1:]:
            whole = whole + pieces[place]
        for place in places:
            sums[place] = whole


def unpack_kernel(rows, reverse, core, back, mine, received, own, send):
    ahead = core[0] == (1 if reverse else 0)
    for head in range(OWNED):
        for part in range(DH // PIECE):
            target = slice(part * PIECE, (part + 1) * PIECE)
            state = back[piece_rows(head * (DH // PIECE) + part, rows)]
            own[head, target] = state + jnp.where(ahead, 0.0, received[head, target])
            send[head, target] = state + jnp.where(ahead, mine[head, target], 0.0)
        if rows > PIECE:
            last = head * (DH // PIECE) * rows + PIECE
            whole = jnp.broadcast_to(back[last:last + 1], (EXTRA, DH))
            own[head, DH:] = whole
            send[head, DH:] = whole


def sums_beyond(core, mine, theirs, seq_size, reverse):
    cores = [(i, i ^ 1) for i in range(seq_size)]
    groups = [[2 * i + one for i in range(seq_size // 2)] for one in range(2)]
    rows = PIECE + (1 if mine.shape[1] > DH else 0)
    flat = (CHIPS * rows, DH)

    def exchange(pieces):
        pieces = pieces.reshape(CHIPS, 1, rows * DH)
        return lax.all_to_all(pieces, "seq", 0, 0, axis_index_groups=groups).reshape(flat)

    received = lax.ppermute(theirs, "seq", cores)
    (pieces,) = call(functools.partial(pack_kernel, rows), "pack", [shape(flat)], core, mine, received)
    (sums,) = call(
        functools.partial(prefix_kernel, rows, reverse), "prefix", [shape(flat)], core, exchange(pieces)
    )
    own, send = call(
        functools.partial(unpack_kernel, rows, reverse), "unpack", [shape(mine.shape)] * 2,
        core, exchange(sums), mine, received,
    )
    return own, lax.ppermute(send, "seq", cores)


def body(queries, keys, values, gate, gain, dout):
    seq_size = lax.axis_size("seq")
    core = lax.rem(lax.axis_index("seq"), 2).astype(jnp.int32).reshape(1)
    gain_row = gain.reshape(1, WIDE)
    half = shape((BLOCK, HALF_WIDE))
    half_low = shape((BLOCK, HALF_WIDE), BF16)
    wide = shape((BLOCK, WIDE), BF16)
    tokens = shape((BLOCK, DH))
    with_gain = shape((OWNED, DH + EXTRA, DH))

    state = shape((OWNED, DH, DH))
    theirs, keys, values = call(
        states_theirs_kernel, "states_theirs", [state, wide, wide], core, keys, values,
        ins=[hbm()] * 2, scratch=[pltpu.SemaphoreType.DMA((2, HEADS_HERE))], limit=8,
    )
    (mine,) = call(states_mine_kernel, "states_mine", [state], core, keys, values)
    own, other = sums_beyond(core, mine, theirs, seq_size, False)
    intra_own, intra_other, normed_own, normed_other = intra_part(core, queries, keys, values, gate, dout)
    out_own, squares, products = call(
        attend_own_kernel, "attend_own", [half, tokens, tokens],
        core, queries, intra_own, normed_own, gain_row, own,
    )
    out_other, sums = call(
        attend_other_kernel, "attend_other", [half, shape((8, DH))],
        core, queries, intra_other, normed_other, gain_row, other, squares, products,
    )
    ring = lax.axis_size("head")
    all_sums = [sums] + [
        lax.ppermute(sums, "head", [(i, (i + step) % ring) for i in range(ring)]) for step in (2, 1, 3)
    ]
    grad_other, scale, cubes, theirs = call(
        grads_theirs_kernel, "grads_theirs", [half_low, tokens, tokens, with_gain],
        core, *all_sums, queries, out_other, normed_other, gain_row,
    )
    grad_own, mine = call(
        grads_mine_kernel, "grads_mine", [half_low, with_gain],
        core, scale, cubes, queries, out_own, normed_own, gain_row,
    )
    buffer = pltpu.VMEM((HEADS_HERE, BLOCK, DH), BF16)
    output, dgate, grad_query, key_own, key_other, value_own, value_other = call(
        local_kernel, "local_grads", [wide, wide, wide, half, half, half, half],
        core, queries, keys, values, gate, out_own, out_other, normed_own, normed_other,
        scale, gain_row, grad_own, grad_other, own, other,
        out_places=[hbm()] * 3 + [vmem()] * 4,
        scratch=[buffer] * 3 + [pltpu.SemaphoreType.DMA((3, HEADS_HERE))],
    )
    own, other = sums_beyond(core, mine, theirs, seq_size, True)
    grad_key, grad_value, dgain = call(
        last_kernel, "last_grads", [wide, wide, shape((HEADS_HERE, DH))],
        core, keys, values, key_own, key_other, value_own, value_other, own, other,
        out_places=[hbm(), hbm(), vmem()],
        scratch=[buffer, buffer, pltpu.SemaphoreType.DMA((2, HEADS_HERE))],
    )
    return output, grad_query, grad_key, grad_value, dgate, dgain.reshape(WIDE)


def solution(mesh):
    wide = P("seq", "head")
    return jax.shard_map(
        body,
        mesh=mesh,
        in_specs=(wide, wide, wide, wide, P("head"), wide),
        out_specs=(wide, wide, wide, wide, wide, P("head")),
        check_vma=False,
    )
```

```python
import functools
import jax
import jax.numpy as jnp
from jax import lax
from jax.experimental import pallas as pl
from jax.experimental.pallas import tpu as pltpu
from jax.sharding import PartitionSpec as P

DH = 128
BLOCK = 512
HALF = BLOCK // 2
HEADS_HERE = 8
OWNED = HEADS_HERE // 2
FEATURES = 4096
COLUMN = 4
ROW = 8
PIECE = OWNED * DH // ROW
EXTRA = 8
EPSILON = 1e-06

F32 = jnp.float32
BF16 = jnp.bfloat16
MIB = 1024 * 1024
FIRST_LIMIT = 8 * MIB
PARTS = 4


def dot_nn(a, b):
    return lax.dot_general(a, b, (((1,), (0,)), ((), ())), preferred_element_type=F32)


def dot_nt(a, b):
    return lax.dot_general(a, b, (((1,), (1,)), ((), ())), preferred_element_type=F32)


def dot_tn(a, b):
    return lax.dot_general(a, b, (((0,), (0,)), ((), ())), preferred_element_type=F32)


def split_state(state):
    high = state.astype(BF16)
    return high, (state - high.astype(F32)).astype(BF16)


def times_state(a, state):
    high, low = split_state(state)
    return dot_nn(jnp.concatenate([a, a], axis=1), jnp.concatenate([high, low], axis=0))


def times_state_t(a, state):
    high, low = split_state(state)
    return dot_nt(jnp.concatenate([a, a], axis=1), jnp.concatenate([high, low], axis=1))


def masked(scores, lower):
    row = lax.broadcasted_iota(jnp.int32, scores.shape, 0)
    column = lax.broadcasted_iota(jnp.int32, scores.shape, 1)
    keep = (row >= column) if lower else (row <= column)
    return jnp.where(keep, scores, 0.0).astype(BF16)


def causal_product(a, b, values):
    top = masked(dot_nt(a[:HALF], b[:HALF]), True)
    left = dot_nt(a[HALF:], b[:HALF]).astype(BF16)
    right = masked(dot_nt(a[HALF:], b[HALF:]), True)
    first = dot_nn(top, values[:HALF])
    second = dot_nn(jnp.concatenate([left, right], axis=1), values)
    return first, second


def anticausal_product(a, b, values):
    left = masked(dot_nt(a[:HALF], b[:HALF]), False)
    right = dot_nt(a[:HALF], b[HALF:]).astype(BF16)
    bottom = masked(dot_nt(a[HALF:], b[HALF:]), False)
    first = dot_nn(jnp.concatenate([left, right], axis=1), values)
    second = dot_nn(bottom, values[HALF:])
    return first, second


WIDE = HEADS_HERE * DH
HALF_WIDE = OWNED * DH


def shape(dims, dtype=F32):
    return jax.ShapeDtypeStruct(dims, dtype)


def vmem():
    return pl.BlockSpec(memory_space=pltpu.VMEM)


def smem():
    return pl.BlockSpec(memory_space=pltpu.SMEM)


def hbm():
    return pl.BlockSpec(memory_space=pltpu.HBM)


def call(kernel, name, outs, core, *args, ins=None, out_places=None, scratch=(), limit=8 * MIB, aliases={}):
    ins = [vmem()] * len(args) if ins is None else ins
    out_places = [vmem()] * len(outs) if out_places is None else out_places
    return pl.pallas_call(
        kernel,
        in_specs=[smem()] + ins,
        out_specs=out_places,
        out_shape=outs,
        scratch_shapes=list(scratch),
        input_output_aliases=aliases,
        compiler_params=pltpu.CompilerParams(vmem_limit_bytes=limit),
        name=name,
    )(core, *args)


def head_columns(core, owned, index):
    first = OWNED * (core[0] if owned else 1 - core[0])
    return pl.ds(pl.multiple_of((first + index) * DH, DH), DH)


def local_columns(index):
    return slice(index * DH, (index + 1) * DH)


def states_kernel(core, column, keys, values, theirs, mine, key_buf, value_buf, sems):
    copies = []
    for part in range(PARTS):
        rows = slice(part * BLOCK // PARTS, (part + 1) * BLOCK // PARTS)
        pair = [
            pltpu.make_async_copy(keys.at[rows], key_buf.at[rows], sems.at[0, part]),
            pltpu.make_async_copy(values.at[rows], value_buf.at[rows], sems.at[1, part]),
        ]
        for copy in pair:
            copy.start()
        copies.append(pair)
    for part in range(PARTS):
        for copy in copies[part]:
            copy.wait()
        rows = slice(part * BLOCK // PARTS, (part + 1) * BLOCK // PARTS)
        for owned, states in ((False, theirs), (True, mine)):
            for index in range(OWNED):
                columns = head_columns(core, owned, index)
                state = dot_tn(key_buf[rows, columns], value_buf[rows, columns])
                states[index] = state if part == 0 else states[index] + state


def intra_kernel(owned, core, queries, keys, values, intra, done):
    for index in range(OWNED):
        columns, here = head_columns(core, owned, index), local_columns(index)
        first, second = causal_product(queries[:, columns], keys[:, columns], values[:, columns])
        intra[:HALF, here] = first
        intra[HALF:, here] = second
    done[...] = jnp.zeros_like(done)


def gates_kernel(core, gate, dout, gain, normed_own, normed_other, gain_here, done):
    for owned, normed in ((True, normed_own), (False, normed_other)):
        for index in range(OWNED):
            columns, here = head_columns(core, owned, index), local_columns(index)
            normed[:, here] = dout[:, columns].astype(F32) * jax.nn.sigmoid(gate[:, columns].astype(F32))
    gain_here[...] = gain[...]
    done[...] = jnp.zeros_like(done)


def turned_kernel(owned, core, queries, keys, top, bottom, done):
    for index in range(OWNED):
        columns = head_columns(core, owned, index)
        query, key = queries[:, columns], keys[:, columns]
        top[index, :, :HALF] = masked(dot_nt(key[:HALF], query[:HALF]), False)
        top[index, :, HALF:] = dot_nt(key[:HALF], query[HALF:]).astype(BF16)
        bottom[index] = masked(dot_nt(key[HALF:], query[HALF:]), False)
    done[...] = jnp.zeros_like(done)


def attend_half(core, owned, queries, intra, normed, gain, state, attn_out):
    squares = products = None
    for index in range(OWNED):
        columns, here = head_columns(core, owned, index), local_columns(index)
        out = intra[:, here] + times_state(queries[:, columns], state[index, :DH])
        attn_out[:, here] = out
        square = out * out
        product = out * (normed[:, here] * gain[:, columns])
        squares = square if squares is None else squares + square
        products = product if products is None else products + product
    return squares, products


def attend_own_kernel(core, queries, intra, normed, gain, state, attn_out, squares, products):
    squares[...], products[...] = attend_half(core, True, queries, intra, normed, gain, state, attn_out)


def attend_other_kernel(core, queries, intra, normed, gain, state, squares, products, attn_out, sums):
    found = attend_half(core, False, queries, intra, normed, gain, state, attn_out)
    for which, (acc, more) in enumerate(zip((squares, products), found)):
        total = acc[...] + more
        for part in range(BLOCK // DH):
            turned = total[part * DH:(part + 1) * DH, :].T
            place = which * (BLOCK // DH) + part
            sums[place:place + 1, :] = jnp.sum(turned, axis=0, keepdims=True)


def grads_half(core, owned, queries, attn_out, normed, gain, scale, cubes, grad, states):
    for index in range(OWNED):
        columns, here = head_columns(core, owned, index), local_columns(index)
        out, rate, one = attn_out[:, here], scale[...], normed[:, here]
        part = (rate * (one * gain[:, columns]) - out * cubes[...]).astype(BF16)
        grad[:, here] = part
        states[index, :DH] = dot_tn(queries[:, columns], part)
        row = jnp.sum(one * out * rate, axis=0, keepdims=True)
        states[index, DH:] = jnp.broadcast_to(row, (EXTRA, DH))


def add_kernel(core, one, other, *done_and_total):
    done_and_total[-1][...] = one[...] + other[...]


def grads_theirs_kernel(core, pair, other_pair, turned_done, early_done, queries, attn_out, normed, gain,
                        grad, scale, cubes, theirs):
    whole = pair[...] + other_pair[...]
    for part in range(BLOCK // DH):
        rows = slice(part * DH, (part + 1) * DH)
        mean_square = whole[part:part + 1, :] / FEATURES
        mean_prod = whole[part + 4:part + 5, :] / FEATURES
        one = lax.rsqrt(mean_square + EPSILON)
        scale[rows, :] = jnp.broadcast_to(one, (DH, DH)).T
        cubes[rows, :] = jnp.broadcast_to(one * one * one * mean_prod, (DH, DH)).T
    grads_half(core, False, queries, attn_out, normed, gain, scale, cubes, grad, theirs)


def grads_mine_kernel(core, scale, cubes, queries, attn_out, normed, gain, grad, mine):
    grads_half(core, True, queries, attn_out, normed, gain, scale, cubes, grad, mine)


def each_head(core, *halves):
    for owned in (True, False):
        for index in range(OWNED):
            place = index if owned else OWNED + index
            arrays = [pair[0] if owned else pair[1] for pair in halves]
            yield head_columns(core, owned, index), local_columns(index), place, index, arrays


def early_kernel(owned, core, gate, attn_out, normed, gain, output, dgate, done):
    for index in range(OWNED):
        columns, here = head_columns(core, owned, index), local_columns(index)
        sig = jax.nn.sigmoid(gate[:, columns].astype(F32))
        scaled = attn_out[:, here] * gain[:, columns]
        output[:, here] = scaled * sig
        dgate[:, here] = normed[:, here] * scaled * (1.0 - sig)
    done[...] = jnp.zeros_like(done)


def outputs_kernel(core, scale, output_own, output_other, dgate_own, dgate_other, output, dgate, done):
    for columns, here, _, _, (early_output, early_dgate) in each_head(
        core, (output_own, output_other), (dgate_own, dgate_other)
    ):
        rate = scale[...]
        output[:, columns] = (early_output[:, here] * rate).astype(BF16)
        dgate[:, columns] = (early_dgate[:, here] * rate).astype(BF16)
    done[...] = jnp.zeros_like(done)


def copy_out(source, target, sem):
    copy = pltpu.make_async_copy(source, target, sem)
    copy.start()
    return copy


def query_kernel(core, keys, values, grad_own, grad_other, own, other, output_here,
                 grad_query, output, done, sem):
    copy = copy_out(output_here, output, sem)
    for columns, here, _, index, (grads, states) in each_head(core, (grad_own, grad_other), (own, other)):
        grad = grads[:, here]
        inter = times_state_t(grad, states[index, :DH])
        first, second = causal_product(grad, values[:, columns], keys[:, columns])
        grad_query[:HALF, columns] = (first + inter[:HALF]).astype(BF16)
        grad_query[HALF:, columns] = (second + inter[HALF:]).astype(BF16)
    done[...] = jnp.zeros_like(done)
    copy.wait()


def key_kernel(core, queries, values, grad_own, grad_other, dgate_here, key_own, key_other, dgate, done, sem):
    copy = copy_out(dgate_here, dgate, sem)
    for columns, here, _, _, (grads, part) in each_head(core, (grad_own, grad_other), (key_own, key_other)):
        first, second = anticausal_product(values[:, columns], grads[:, here], queries[:, columns])
        part[:HALF, here] = first
        part[HALF:, here] = second
    done[...] = jnp.zeros_like(done)
    copy.wait()


def value_kernel(core, grad_own, grad_other, top_own, top_other, bottom_own, bottom_other, query_here,
                 value_own, value_other, grad_query, sem):
    copy = copy_out(query_here, grad_query, sem)
    for _, here, _, index, (grads, top, bottom, part) in each_head(
        core, (grad_own, grad_other), (top_own, top_other), (bottom_own, bottom_other), (value_own, value_other)
    ):
        part[:HALF, here] = dot_nn(top[index], grads[:, here])
        part[HALF:, here] = dot_nn(bottom[index], grads[HALF:, here])
    copy.wait()


def last_half(owned, core, keys, values, part_key, part_value, states, grad_key, grad_value, key_buf, value_buf, sems):
    copies = []
    for index in range(OWNED):
        columns, here = head_columns(core, owned, index), local_columns(index)
        state = states[index, :DH]
        key_buf[index] = (part_key[:, here] + times_state_t(values[:, columns], state)).astype(BF16)
        value_buf[index] = (part_value[:, here] + times_state(keys[:, columns], state)).astype(BF16)
        for which, (buffer, target) in enumerate(((key_buf, grad_key), (value_buf, grad_value))):
            copy = pltpu.make_async_copy(buffer.at[index], target.at[:, columns], sems.at[which, index])
            copy.start()
            copies.append(copy)
    for copy in copies:
        copy.wait()


def last_own_kernel(core, keys, values, part_key, part_value, states, grad_key, grad_value, *scratch):
    last_half(True, core, keys, values, part_key, part_value, states, grad_key, grad_value, *scratch)


def last_other_kernel(core, keys, values, part_key, part_value, own, other, key_before, value_before,
                      grad_key, grad_value, dgain, dgain_buf, dgain_sem, *scratch):
    for owned, states in ((True, own), (False, other)):
        for index in range(OWNED):
            row = OWNED * (core[0] if owned else 1 - core[0]) + index
            dgain_buf[pl.ds(row, 1), :] = states[index, DH:DH + 1]
    copy = pltpu.make_async_copy(dgain_buf, dgain, dgain_sem)
    copy.start()
    last_half(False, core, keys, values, part_key, part_value, other, grad_key, grad_value, *scratch)
    copy.wait()


def piece_rows(place, rows):
    return slice(place * rows, place * rows + PIECE)


def pack_kernel(rows, reverse, core, mine, received, *done_and_results):
    *_, pieces, kept = done_and_results
    ahead = core[0] == (1 if reverse else 0)
    for head in range(OWNED):
        kept[head] = jnp.where(ahead, mine[head, :DH], received[head, :DH])
    for head in range(OWNED):
        for part in range(DH // PIECE):
            source = slice(part * PIECE, (part + 1) * PIECE)
            place = head * (DH // PIECE) + part
            pieces[piece_rows(place, rows)] = mine[head, source] + received[head, source]
            if rows > PIECE:
                last = place * rows + PIECE
                pieces[last:last + 1] = mine[head, DH:DH + 1] + received[head, DH:DH + 1]


def row_total_kernel(rows, core, pieces, total):
    whole = pieces[:rows]
    for chip in range(1, ROW):
        whole = whole + pieces[chip * rows:(chip + 1) * rows]
    total[...] = whole


def prefix_kernel(rows, reverse, column, pieces, neighbour, pair, other_pair, *done_and_sums):
    sums = done_and_sums[-1]
    odd, high = lax.rem(column[0], 2) == 1, column[0] >= 2
    take_one = jnp.logical_not(odd) if reverse else odd
    take_pair = jnp.logical_not(high) if reverse else high
    total = jnp.where(take_one, neighbour[:PIECE], 0.0) + jnp.where(take_pair, other_pair[:PIECE], 0.0)
    order = range(ROW - 1, -1, -1) if reverse else range(ROW)
    for chip in order:
        sums[piece_rows(chip, rows)] = total
        total = total + pieces[piece_rows(chip, rows)]
    if rows > PIECE:
        whole = pair[PIECE:] + other_pair[PIECE:]
        for chip in range(ROW):
            sums[chip * rows + PIECE:(chip + 1) * rows] = whole


def unpack_kernel(rows, reverse, core, back, kept, own, send):
    ahead = core[0] == (1 if reverse else 0)
    for head in range(OWNED):
        for part in range(DH // PIECE):
            target = slice(part * PIECE, (part + 1) * PIECE)
            state = back[piece_rows(head * (DH // PIECE) + part, rows)]
            both = state + kept[head, target]
            own[head, target] = jnp.where(ahead, state, both)
            send[head, target] = jnp.where(ahead, both, state)
        if rows > PIECE:
            last = head * (DH // PIECE) * rows + PIECE
            whole = jnp.broadcast_to(back[last:last + 1], (EXTRA, DH))
            own[head, DH:] = whole
            send[head, DH:] = whole


def device(column, row, core):
    return (column * ROW + row) * 2 + core


def moved(to_column):
    return [
        (device(y, z, c), device(to_column(y), z, c))
        for y in range(COLUMN) for z in range(ROW) for c in range(2)
    ]


CORES = [(i, i ^ 1) for i in range(2 * COLUMN * ROW)]
ROWS = [[device(y, z, c) for z in range(ROW)] for y in range(COLUMN) for c in range(2)]


def sums_beyond(core, column, mine, theirs, reverse, beside_first, beside_second, before=()):
    rows = PIECE + (1 if mine.shape[1] > DH else 0)
    flat = (ROW * rows, DH)

    def exchange(pieces):
        pieces = pieces.reshape(ROW, 1, rows * DH)
        return lax.all_to_all(pieces, "seq", 0, 0, axis_index_groups=ROWS).reshape(flat)

    received = lax.ppermute(theirs, "seq", CORES)
    pieces, kept = call(
        functools.partial(pack_kernel, rows, reverse), "pack", [shape(flat), shape((OWNED, DH, DH))],
        core, mine, received, *before,
    )
    pieces = exchange(pieces)
    (total,) = call(functools.partial(row_total_kernel, rows), "row_total", [shape((rows, DH))], core, pieces)
    neighbour = lax.ppermute(total, "seq", moved(lambda y: y ^ 1))
    first = beside_first()
    (pair,) = call(add_kernel, "pair_total", [shape((rows, DH))], core, total, neighbour, first)
    other_pair = lax.ppermute(pair, "seq", moved(lambda y: COLUMN - 1 - y))
    second = beside_second()
    (sums,) = call(
        functools.partial(prefix_kernel, rows, reverse), "prefix", [shape(flat)],
        column, pieces, neighbour, pair, other_pair, *second,
    )
    own, send = call(
        functools.partial(unpack_kernel, rows, reverse), "unpack", [shape(mine.shape)] * 2,
        core, exchange(sums), kept,
    )
    return own, lax.ppermute(send, "seq", CORES)


def body(queries, keys, values, gate, gain, dout):
    index = lax.axis_index("seq").astype(jnp.int32)
    core = lax.rem(index, 2).reshape(1)
    column = lax.div(index, 2 * ROW).reshape(1)
    gain_row = gain.reshape(1, WIDE)
    half = shape((BLOCK, HALF_WIDE))
    half_low = shape((BLOCK, HALF_WIDE), BF16)
    wide = shape((BLOCK, WIDE), BF16)
    tokens = shape((BLOCK, DH))
    with_gain = shape((OWNED, DH + EXTRA, DH))
    done = shape((8, DH))

    state = shape((OWNED, DH, DH))
    whole = pltpu.VMEM((BLOCK, WIDE), BF16)
    theirs, mine = call(
        states_kernel, "states", [state, state], core, column, keys, values,
        ins=[smem()] + [hbm()] * 2,
        scratch=[whole, whole, pltpu.SemaphoreType.DMA((2, PARTS))],
        limit=FIRST_LIMIT,
    )

    intra = {}

    def intra_part(owned):
        name = "intra_own" if owned else "intra_other"
        intra[owned], ended = call(
            functools.partial(intra_kernel, owned), name, [half, done], core, queries, keys, values,
        )
        return ended

    normed_own, normed_other, gain_row, gates_done = call(
        gates_kernel, "gates", [half, half, shape((1, WIDE)), done], core, gate, dout, gain_row,
    )
    own, other = sums_beyond(
        core, column, mine, theirs, False,
        lambda: intra_part(True), lambda: (intra_part(False), gates_done),
    )
    intra_own, intra_other = intra[True], intra[False]
    out_own, squares, products = call(
        attend_own_kernel, "attend_own", [half, tokens, tokens],
        core, queries, intra_own, normed_own, gain_row, own,
    )
    out_other, sums = call(
        attend_other_kernel, "attend_other", [half, done],
        core, queries, intra_other, normed_other, gain_row, other, squares, products,
    )

    turned = {}

    def turned_part(owned):
        name = "turned_own" if owned else "turned_other"
        *turned[owned], ended = call(
            functools.partial(turned_kernel, owned), name,
            [shape((OWNED, HALF, BLOCK), BF16), shape((OWNED, HALF, HALF), BF16), done],
            core, queries, keys,
        )
        return ended

    early = {}

    def early_part(owned, attn_out, normed):
        name = "early_own" if owned else "early_other"
        *early[owned], ended = call(
            functools.partial(early_kernel, owned), name, [half, half, done],
            core, gate, attn_out, normed, gain_row,
        )
        return ended

    ring = lax.axis_size("head")
    neighbour = lax.ppermute(sums, "head", [(i, i ^ 1) for i in range(ring)])
    (pair,) = call(
        add_kernel, "pair_sums", [done],
        core, sums, neighbour, turned_part(True), early_part(True, out_own, normed_own),
    )
    other_pair = lax.ppermute(pair, "head", [(i, ring - 1 - i) for i in range(ring)])
    grad_other, scale, cubes, theirs = call(
        grads_theirs_kernel, "grads_theirs", [half_low, tokens, tokens, with_gain],
        core, pair, other_pair, turned_part(False), early_part(False, out_other, normed_other),
        queries, out_other, normed_other, gain_row,
    )
    grad_own, mine = call(
        grads_mine_kernel, "grads_mine", [half_low, with_gain],
        core, scale, cubes, queries, out_own, normed_own, gain_row,
    )
    output, dgate, outputs_done = call(
        outputs_kernel, "outputs", [wide, wide, done],
        core, scale, early[True][0], early[False][0], early[True][1], early[False][1],
    )

    results = {}

    one_copy = [pltpu.SemaphoreType.DMA]

    def query_part():
        *results["query"], ended = call(
            query_kernel, "grad_query", [wide, wide, done],
            core, keys, values, grad_own, grad_other, own, other, output,
            out_places=[vmem(), hbm(), vmem()],
            scratch=one_copy,
        )
        return ended

    def key_part():
        *results["key"], ended = call(
            key_kernel, "grad_key", [half, half, wide, done],
            core, queries, values, grad_own, grad_other, dgate,
            out_places=[vmem(), vmem(), hbm(), vmem()],
            scratch=one_copy,
        )
        return (ended,)

    later_own, later_other = sums_beyond(
        core, column, mine, theirs, True, query_part, key_part, (outputs_done,)
    )
    grad_query, output = results["query"]
    key_own, key_other, dgate = results["key"]
    value_own, value_other, grad_query = call(
        value_kernel, "grad_value", [half, half, wide],
        core, grad_own, grad_other, turned[True][0], turned[False][0], turned[True][1], turned[False][1],
        grad_query,
        out_places=[vmem(), vmem(), hbm()],
        scratch=one_copy,
    )
    buffer = pltpu.VMEM((OWNED, BLOCK, DH), BF16)
    scratch = [buffer, buffer, pltpu.SemaphoreType.DMA((2, OWNED))]
    grad_key, grad_value = call(
        last_own_kernel, "last_own", [wide, wide], core, keys, values, key_own, value_own, later_own,
        out_places=[hbm(), hbm()],
        scratch=scratch,
    )
    grad_key, grad_value, dgain = call(
        last_other_kernel, "last_other", [wide, wide, shape((HEADS_HERE, DH))],
        core, keys, values, key_other, value_other, later_own, later_other, grad_key, grad_value,
        ins=[vmem()] * 6 + [hbm()] * 2,
        out_places=[hbm()] * 3,
        scratch=[pltpu.VMEM((HEADS_HERE, DH), F32), pltpu.SemaphoreType.DMA] + scratch,
        aliases={7: 0, 8: 1},
    )
    return output, grad_query, grad_key, grad_value, dgate, dgain.reshape(WIDE)


def solution(mesh):
    wide = P("seq", "head")
    return jax.shard_map(
        body,
        mesh=mesh,
        in_specs=(wide, wide, wide, wide, P("head"), wide),
        out_specs=(wide, wide, wide, wide, wide, P("head")),
        check_vma=False,
    )
```

```python
import functools
import jax
import jax.numpy as jnp
from jax import lax
from jax.experimental import pallas as pl
from jax.experimental.pallas import tpu as pltpu
from jax.sharding import PartitionSpec as P

DH = 128
BLOCK = 512
HALF = BLOCK // 2
HEADS_HERE = 8
OWNED = HEADS_HERE // 2
FEATURES = 4096
COLUMN = 4
ROW = 8
PIECE = OWNED * DH // ROW
EXTRA = 8
EPSILON = 1e-06

F32 = jnp.float32
BF16 = jnp.bfloat16
MIB = 1024 * 1024


def dot_nn(a, b):
    return lax.dot_general(a, b, (((1,), (0,)), ((), ())), preferred_element_type=F32)


def dot_nt(a, b):
    return lax.dot_general(a, b, (((1,), (1,)), ((), ())), preferred_element_type=F32)


def dot_tn(a, b):
    return lax.dot_general(a, b, (((0,), (0,)), ((), ())), preferred_element_type=F32)


def split_state(state):
    high = state.astype(BF16)
    return high, (state - high.astype(F32)).astype(BF16)


def times_state(a, state):
    high, low = split_state(state)
    return dot_nn(jnp.concatenate([a, a], axis=1), jnp.concatenate([high, low], axis=0))


def times_state_t(a, state):
    high, low = split_state(state)
    return dot_nt(jnp.concatenate([a, a], axis=1), jnp.concatenate([high, low], axis=1))


def masked(scores, lower):
    row = lax.broadcasted_iota(jnp.int32, scores.shape, 0)
    column = lax.broadcasted_iota(jnp.int32, scores.shape, 1)
    keep = (row >= column) if lower else (row <= column)
    return jnp.where(keep, scores, 0.0).astype(BF16)


def causal_product(a, b, values):
    top = masked(dot_nt(a[:HALF], b[:HALF]), True)
    left = dot_nt(a[HALF:], b[:HALF]).astype(BF16)
    right = masked(dot_nt(a[HALF:], b[HALF:]), True)
    first = dot_nn(top, values[:HALF])
    second = dot_nn(jnp.concatenate([left, right], axis=1), values)
    return first, second


def anticausal_product(a, b, values):
    left = masked(dot_nt(a[:HALF], b[:HALF]), False)
    right = dot_nt(a[:HALF], b[HALF:]).astype(BF16)
    bottom = masked(dot_nt(a[HALF:], b[HALF:]), False)
    first = dot_nn(jnp.concatenate([left, right], axis=1), values)
    second = dot_nn(bottom, values[HALF:])
    return first, second


WIDE = HEADS_HERE * DH
HALF_WIDE = OWNED * DH


def shape(dims, dtype=F32):
    return jax.ShapeDtypeStruct(dims, dtype)


def vmem():
    return pl.BlockSpec(memory_space=pltpu.VMEM)


def smem():
    return pl.BlockSpec(memory_space=pltpu.SMEM)


def hbm():
    return pl.BlockSpec(memory_space=pltpu.HBM)


def call(kernel, name, outs, core, *args, ins=None, out_places=None, scratch=(), limit=8 * MIB, aliases={}):
    ins = [vmem()] * len(args) if ins is None else ins
    out_places = [vmem()] * len(outs) if out_places is None else out_places
    return pl.pallas_call(
        kernel,
        in_specs=[smem()] + ins,
        out_specs=out_places,
        out_shape=outs,
        scratch_shapes=list(scratch),
        input_output_aliases=aliases,
        compiler_params=pltpu.CompilerParams(vmem_limit_bytes=limit),
        name=name,
    )(core, *args)


def head_columns(core, owned, index):
    first = OWNED * (core[0] if owned else 1 - core[0])
    return pl.ds(pl.multiple_of((first + index) * DH, DH), DH)


def local_columns(index):
    return slice(index * DH, (index + 1) * DH)


def turn_keys_kernel(core, column, keys, turned):
    for head in range(HEADS_HERE):
        columns = local_columns(head)
        turned[head] = keys[:, columns].T


def states_kernel(core, turned, values, theirs, mine):
    for owned, states in ((False, theirs), (True, mine)):
        for index in range(OWNED):
            head = OWNED * (core[0] if owned else 1 - core[0]) + index
            states[index] = dot_nn(turned[head], values[:, head_columns(core, owned, index)])


def intra_kernel(owned, core, queries, keys, values, intra, done):
    for index in range(OWNED):
        columns, here = head_columns(core, owned, index), local_columns(index)
        first, second = causal_product(queries[:, columns], keys[:, columns], values[:, columns])
        intra[:HALF, here] = first
        intra[HALF:, here] = second
    done[...] = jnp.zeros_like(done)


def gates_kernel(core, gate, dout, gain, normed_own, normed_other, gain_here, done):
    for owned, normed in ((True, normed_own), (False, normed_other)):
        for index in range(OWNED):
            columns, here = head_columns(core, owned, index), local_columns(index)
            normed[:, here] = dout[:, columns].astype(F32) * jax.nn.sigmoid(gate[:, columns].astype(F32))
    gain_here[...] = gain[...]
    done[...] = jnp.zeros_like(done)


def turned_kernel(owned, core, queries, keys, top, bottom, done):
    for index in range(OWNED):
        columns = head_columns(core, owned, index)
        query, key = queries[:, columns], keys[:, columns]
        top[index, :, :HALF] = masked(dot_nt(key[:HALF], query[:HALF]), False)
        top[index, :, HALF:] = dot_nt(key[:HALF], query[HALF:]).astype(BF16)
        bottom[index] = masked(dot_nt(key[HALF:], query[HALF:]), False)
    done[...] = jnp.zeros_like(done)


def attend_half(core, owned, queries, intra, normed, gain, state, attn_out):
    squares = products = None
    for index in range(OWNED):
        columns, here = head_columns(core, owned, index), local_columns(index)
        out = intra[:, here] + times_state(queries[:, columns], state[index, :DH])
        attn_out[:, here] = out
        square = out * out
        product = out * (normed[:, here] * gain[:, columns])
        squares = square if squares is None else squares + square
        products = product if products is None else products + product
    return squares, products


def attend_own_kernel(core, queries, intra, normed, gain, state, attn_out, squares, products):
    squares[...], products[...] = attend_half(core, True, queries, intra, normed, gain, state, attn_out)


def attend_other_kernel(core, queries, intra, normed, gain, state, squares, products, attn_out, sums):
    found = attend_half(core, False, queries, intra, normed, gain, state, attn_out)
    for which, (acc, more) in enumerate(zip((squares, products), found)):
        total = acc[...] + more
        for part in range(BLOCK // DH):
            turned = total[part * DH:(part + 1) * DH, :].T
            place = which * (BLOCK // DH) + part
            sums[place:place + 1, :] = jnp.sum(turned, axis=0, keepdims=True)


def grads_half(core, owned, queries, attn_out, normed, gain, scale, cubes, grad, states):
    for index in range(OWNED):
        columns, here = head_columns(core, owned, index), local_columns(index)
        out, rate, one = attn_out[:, here], scale[...], normed[:, here]
        part = (rate * (one * gain[:, columns]) - out * cubes[...]).astype(BF16)
        grad[:, here] = part
        states[index, :DH] = dot_tn(queries[:, columns], part)
        row = jnp.sum(one * out * rate, axis=0, keepdims=True)
        states[index, DH:] = jnp.broadcast_to(row, (EXTRA, DH))


def add_kernel(core, one, other, *done_and_total):
    done_and_total[-1][...] = one[...] + other[...]


def grads_theirs_kernel(core, pair, other_pair, turned_done, early_done, queries, attn_out, normed, gain,
                        grad, scale, cubes, theirs):
    whole = pair[...] + other_pair[...]
    for part in range(BLOCK // DH):
        rows = slice(part * DH, (part + 1) * DH)
        mean_square = whole[part:part + 1, :] / FEATURES
        mean_prod = whole[part + 4:part + 5, :] / FEATURES
        one = lax.rsqrt(mean_square + EPSILON)
        scale[rows, :] = jnp.broadcast_to(one, (DH, DH)).T
        cubes[rows, :] = jnp.broadcast_to(one * one * one * mean_prod, (DH, DH)).T
    grads_half(core, False, queries, attn_out, normed, gain, scale, cubes, grad, theirs)


def grads_mine_kernel(core, scale, cubes, queries, attn_out, normed, gain, grad, mine):
    grads_half(core, True, queries, attn_out, normed, gain, scale, cubes, grad, mine)


def each_head(core, *halves):
    for owned in (True, False):
        for index in range(OWNED):
            place = index if owned else OWNED + index
            arrays = [pair[0] if owned else pair[1] for pair in halves]
            yield head_columns(core, owned, index), local_columns(index), place, index, arrays


def early_kernel(owned, core, gate, attn_out, normed, gain, output, dgate, done):
    for index in range(OWNED):
        columns, here = head_columns(core, owned, index), local_columns(index)
        sig = jax.nn.sigmoid(gate[:, columns].astype(F32))
        scaled = attn_out[:, here] * gain[:, columns]
        output[:, here] = scaled * sig
        dgate[:, here] = normed[:, here] * scaled * (1.0 - sig)
    done[...] = jnp.zeros_like(done)


def outputs_kernel(core, scale, output_own, output_other, dgate_own, dgate_other, output, dgate, done):
    for columns, here, _, _, (early_output, early_dgate) in each_head(
        core, (output_own, output_other), (dgate_own, dgate_other)
    ):
        rate = scale[...]
        output[:, columns] = (early_output[:, here] * rate).astype(BF16)
        dgate[:, columns] = (early_dgate[:, here] * rate).astype(BF16)
    done[...] = jnp.zeros_like(done)


def copy_out(source, target, sem):
    copy = pltpu.make_async_copy(source, target, sem)
    copy.start()
    return copy


def query_kernel(core, keys, values, grad_own, grad_other, own, other, output_here,
                 grad_query, output, done, sem):
    copy = copy_out(output_here, output, sem)
    for columns, here, _, index, (grads, states) in each_head(core, (grad_own, grad_other), (own, other)):
        grad = grads[:, here]
        inter = times_state_t(grad, states[index, :DH])
        first, second = causal_product(grad, values[:, columns], keys[:, columns])
        grad_query[:HALF, columns] = (first + inter[:HALF]).astype(BF16)
        grad_query[HALF:, columns] = (second + inter[HALF:]).astype(BF16)
    done[...] = jnp.zeros_like(done)
    copy.wait()


def key_kernel(core, queries, values, grad_own, grad_other, dgate_here, key_own, key_other, dgate, done, sem):
    copy = copy_out(dgate_here, dgate, sem)
    for columns, here, _, _, (grads, part) in each_head(core, (grad_own, grad_other), (key_own, key_other)):
        first, second = anticausal_product(values[:, columns], grads[:, here], queries[:, columns])
        part[:HALF, here] = first
        part[HALF:, here] = second
    done[...] = jnp.zeros_like(done)
    copy.wait()


def value_kernel(core, grad_own, grad_other, top_own, top_other, bottom_own, bottom_other, query_here,
                 value_own, value_other, grad_query, done, sem):
    copy = copy_out(query_here, grad_query, sem)
    for _, here, _, index, (grads, top, bottom, part) in each_head(
        core, (grad_own, grad_other), (top_own, top_other), (bottom_own, bottom_other), (value_own, value_other)
    ):
        part[:HALF, here] = dot_nn(top[index], grads[:, here])
        part[HALF:, here] = dot_nn(bottom[index], grads[HALF:, here])
    done[...] = jnp.zeros_like(done)
    copy.wait()


def last_half(owned, core, keys, values, part_key, part_value, states, grad_key, grad_value, key_buf, value_buf, sems):
    copies = []
    for index in range(OWNED):
        columns, here = head_columns(core, owned, index), local_columns(index)
        state = states[index, :DH]
        key_buf[index] = (part_key[:, here] + times_state_t(values[:, columns], state)).astype(BF16)
        value_buf[index] = (part_value[:, here] + times_state(keys[:, columns], state)).astype(BF16)
        for which, (buffer, target) in enumerate(((key_buf, grad_key), (value_buf, grad_value))):
            copy = pltpu.make_async_copy(buffer.at[index], target.at[:, columns], sems.at[which, index])
            copy.start()
            copies.append(copy)
    for copy in copies:
        copy.wait()


def last_own_kernel(core, keys, values, part_key, part_value, states, grad_key, grad_value, *scratch):
    last_half(True, core, keys, values, part_key, part_value, states, grad_key, grad_value, *scratch)


def last_other_kernel(core, keys, values, part_key, part_value, own, other, key_before, value_before,
                      grad_key, grad_value, dgain, dgain_buf, dgain_sem, *scratch):
    for owned, states in ((True, own), (False, other)):
        for index in range(OWNED):
            row = OWNED * (core[0] if owned else 1 - core[0]) + index
            dgain_buf[pl.ds(row, 1), :] = states[index, DH:DH + 1]
    copy = pltpu.make_async_copy(dgain_buf, dgain, dgain_sem)
    copy.start()
    last_half(False, core, keys, values, part_key, part_value, other, grad_key, grad_value, *scratch)
    copy.wait()


def piece_rows(place, rows):
    return slice(place * rows, place * rows + PIECE)


def pack_kernel(rows, reverse, core, mine, received, *done_and_results):
    *_, pieces, kept = done_and_results
    ahead = core[0] == (1 if reverse else 0)
    for head in range(OWNED):
        kept[head] = jnp.where(ahead, mine[head, :DH], received[head, :DH])
    for head in range(OWNED):
        for part in range(DH // PIECE):
            source = slice(part * PIECE, (part + 1) * PIECE)
            place = head * (DH // PIECE) + part
            pieces[piece_rows(place, rows)] = mine[head, source] + received[head, source]
    if rows > PIECE:
        gains = [mine[head, DH:DH + 1] + received[head, DH:DH + 1] for head in range(OWNED)]
        for place in range(ROW):
            pieces[place * rows + PIECE:(place + 1) * rows] = jnp.concatenate(gains, axis=0)


def row_total_kernel(rows, core, pieces, total):
    whole = pieces[:rows]
    for chip in range(1, ROW):
        whole = whole + pieces[chip * rows:(chip + 1) * rows]
    total[...] = whole


def prefix_kernel(rows, reverse, column, pieces, neighbour, pair, other_pair, *done_and_results):
    *_, sums, gains = done_and_results
    odd, high = lax.rem(column[0], 2) == 1, column[0] >= 2
    take_one = jnp.logical_not(odd) if reverse else odd
    take_pair = jnp.logical_not(high) if reverse else high
    total = jnp.where(take_one, neighbour[:PIECE], 0.0) + jnp.where(take_pair, other_pair[:PIECE], 0.0)
    order = range(ROW - 1, -1, -1) if reverse else range(ROW)
    for chip in order:
        sums[piece_rows(chip, PIECE)] = total
        total = total + pieces[piece_rows(chip, rows)]
    if rows > PIECE:
        gains[:OWNED] = pair[PIECE:] + other_pair[PIECE:]


def unpack_kernel(rows, reverse, core, back, kept, gains, own, send):
    ahead = core[0] == (1 if reverse else 0)
    for head in range(OWNED):
        for part in range(DH // PIECE):
            target = slice(part * PIECE, (part + 1) * PIECE)
            state = back[piece_rows(head * (DH // PIECE) + part, PIECE)]
            both = state + kept[head, target]
            own[head, target] = jnp.where(ahead, state, both)
            send[head, target] = jnp.where(ahead, both, state)
        if rows > PIECE:
            whole = jnp.broadcast_to(gains[head:head + 1], (EXTRA, DH))
            own[head, DH:] = whole
            send[head, DH:] = whole


def device(column, row, core):
    return (column * ROW + row) * 2 + core


def moved(to_column):
    return [
        (device(y, z, c), device(to_column(y), z, c))
        for y in range(COLUMN) for z in range(ROW) for c in range(2)
    ]


CORES = [(i, i ^ 1) for i in range(2 * COLUMN * ROW)]
ROWS = [[device(y, z, c) for z in range(ROW)] for y in range(COLUMN) for c in range(2)]


def sums_beyond(core, column, mine, theirs, reverse, beside_first, beside_second, before=()):
    rows = PIECE + (OWNED if mine.shape[1] > DH else 0)

    def exchange(pieces):
        high = pieces.shape[0]
        pieces = pieces.reshape(ROW, 1, high // ROW * DH)
        return lax.all_to_all(pieces, "seq", 0, 0, axis_index_groups=ROWS).reshape(high, DH)

    received = lax.ppermute(theirs, "seq", CORES)
    pieces, kept = call(
        functools.partial(pack_kernel, rows, reverse), "pack", [shape((ROW * rows, DH)), shape((OWNED, DH, DH))],
        core, mine, received, *before,
    )
    pieces = exchange(pieces)
    (total,) = call(functools.partial(row_total_kernel, rows), "row_total", [shape((rows, DH))], core, pieces)
    neighbour = lax.ppermute(total, "seq", moved(lambda y: y ^ 1))
    first = beside_first()
    (pair,) = call(add_kernel, "pair_total", [shape((rows, DH))], core, total, neighbour, first)
    other_pair = lax.ppermute(pair, "seq", moved(lambda y: COLUMN - 1 - y))
    second = beside_second()
    sums, gains = call(
        functools.partial(prefix_kernel, rows, reverse), "prefix", [shape((ROW * PIECE, DH)), shape((8, DH))],
        column, pieces, neighbour, pair, other_pair, *second,
    )
    own, send = call(
        functools.partial(unpack_kernel, rows, reverse), "unpack", [shape(mine.shape)] * 2,
        core, exchange(sums), kept, gains,
    )
    return own, lax.ppermute(send, "seq", CORES)


def body(queries, keys, values, gate, gain, dout):
    index = lax.axis_index("seq").astype(jnp.int32)
    core = lax.rem(index, 2).reshape(1)
    column = lax.div(index, 2 * ROW).reshape(1)
    gain_row = gain.reshape(1, WIDE)
    half = shape((BLOCK, HALF_WIDE))
    half_low = shape((BLOCK, HALF_WIDE), BF16)
    wide = shape((BLOCK, WIDE), BF16)
    tokens = shape((BLOCK, DH))
    with_gain = shape((OWNED, DH + EXTRA, DH))
    done = shape((8, DH))

    state = shape((OWNED, DH, DH))
    (turned_keys,) = call(
        turn_keys_kernel, "turn_keys", [shape((HEADS_HERE, DH, BLOCK), BF16)], core, column, keys,
        ins=[smem(), vmem()],
    )
    theirs, mine = call(states_kernel, "states", [state, state], core, turned_keys, values)

    intra = {}

    def intra_part(owned):
        name = "intra_own" if owned else "intra_other"
        intra[owned], ended = call(
            functools.partial(intra_kernel, owned), name, [half, done], core, queries, keys, values,
        )
        return ended

    normed_own, normed_other, gain_row, gates_done = call(
        gates_kernel, "gates", [half, half, shape((1, WIDE)), done], core, gate, dout, gain_row,
    )
    own, other = sums_beyond(
        core, column, mine, theirs, False,
        lambda: intra_part(True), lambda: (intra_part(False), gates_done),
    )
    intra_own, intra_other = intra[True], intra[False]
    out_own, squares, products = call(
        attend_own_kernel, "attend_own", [half, tokens, tokens],
        core, queries, intra_own, normed_own, gain_row, own,
    )
    out_other, sums = call(
        attend_other_kernel, "attend_other", [half, done],
        core, queries, intra_other, normed_other, gain_row, other, squares, products,
    )

    turned = {}

    def turned_part(owned):
        name = "turned_own" if owned else "turned_other"
        *turned[owned], ended = call(
            functools.partial(turned_kernel, owned), name,
            [shape((OWNED, HALF, BLOCK), BF16), shape((OWNED, HALF, HALF), BF16), done],
            core, queries, keys,
        )
        return ended

    early = {}

    def early_part(owned, attn_out, normed):
        name = "early_own" if owned else "early_other"
        *early[owned], ended = call(
            functools.partial(early_kernel, owned), name, [half, half, done],
            core, gate, attn_out, normed, gain_row,
        )
        return ended

    ring = lax.axis_size("head")
    neighbour = lax.ppermute(sums, "head", [(i, i ^ 1) for i in range(ring)])
    (pair,) = call(
        add_kernel, "pair_sums", [done],
        core, sums, neighbour, turned_part(True), early_part(True, out_own, normed_own),
    )
    other_pair = lax.ppermute(pair, "head", [(i, ring - 1 - i) for i in range(ring)])
    grad_other, scale, cubes, theirs = call(
        grads_theirs_kernel, "grads_theirs", [half_low, tokens, tokens, with_gain],
        core, pair, other_pair, turned_part(False), early_part(False, out_other, normed_other),
        queries, out_other, normed_other, gain_row,
    )
    grad_own, mine = call(
        grads_mine_kernel, "grads_mine", [half_low, with_gain],
        core, scale, cubes, queries, out_own, normed_own, gain_row,
    )
    output, dgate, outputs_done = call(
        outputs_kernel, "outputs", [wide, wide, done],
        core, scale, early[True][0], early[False][0], early[True][1], early[False][1],
    )

    results = {}

    one_copy = [pltpu.SemaphoreType.DMA]

    def query_part():
        *results["query"], ended = call(
            query_kernel, "grad_query", [wide, wide, done],
            core, keys, values, grad_own, grad_other, own, other, output,
            out_places=[vmem(), hbm(), vmem()],
            scratch=one_copy,
        )
        return ended

    def key_part():
        *results["key"], ended = call(
            key_kernel, "grad_key", [half, half, wide, done],
            core, queries, values, grad_own, grad_other, dgate,
            out_places=[vmem(), vmem(), hbm(), vmem()],
            scratch=one_copy,
        )
        return ended

    def value_part():
        *results["value"], ended = call(
            value_kernel, "grad_value", [half, half, wide, done],
            core, grad_own, grad_other, turned[True][0], turned[False][0], turned[True][1], turned[False][1],
            results["query"][0],
            out_places=[vmem(), vmem(), hbm(), vmem()],
            scratch=one_copy,
        )
        return ended

    later_own, later_other = sums_beyond(
        core, column, mine, theirs, True, query_part, lambda: (key_part(), value_part()), (outputs_done,)
    )
    output = results["query"][1]
    key_own, key_other, dgate = results["key"]
    value_own, value_other, grad_query = results["value"]
    buffer = pltpu.VMEM((OWNED, BLOCK, DH), BF16)
    scratch = [buffer, buffer, pltpu.SemaphoreType.DMA((2, OWNED))]
    grad_key, grad_value = call(
        last_own_kernel, "last_own", [wide, wide], core, keys, values, key_own, value_own, later_own,
        out_places=[hbm(), hbm()],
        scratch=scratch,
    )
    grad_key, grad_value, dgain = call(
        last_other_kernel, "last_other", [wide, wide, shape((HEADS_HERE, DH))],
        core, keys, values, key_other, value_other, later_own, later_other, grad_key, grad_value,
        ins=[vmem()] * 6 + [hbm()] * 2,
        out_places=[hbm()] * 3,
        scratch=[pltpu.VMEM((HEADS_HERE, DH), F32), pltpu.SemaphoreType.DMA] + scratch,
        aliases={7: 0, 8: 1},
    )
    return output, grad_query, grad_key, grad_value, dgate, dgain.reshape(WIDE)


def solution(mesh):
    wide = P("seq", "head")
    return jax.shard_map(
        body,
        mesh=mesh,
        in_specs=(wide, wide, wide, wide, P("head"), wide),
        out_specs=(wide, wide, wide, wide, wide, P("head")),
        check_vma=False,
    )
```

```python
import functools
import jax
import jax.numpy as jnp
from jax import lax
from jax.experimental import pallas as pl
from jax.experimental.pallas import tpu as pltpu
from jax.sharding import PartitionSpec as P

DH = 128
BLOCK = 512
HALF = BLOCK // 2
HEADS_HERE = 8
OWNED = HEADS_HERE // 2
FEATURES = 4096
COLUMN = 4
ROW = 8
PIECE = OWNED * DH // ROW
EXTRA = 8
EPSILON = 1e-06

F32 = jnp.float32
BF16 = jnp.bfloat16
MIB = 1024 * 1024


def dot_nn(a, b):
    return lax.dot_general(a, b, (((1,), (0,)), ((), ())), preferred_element_type=F32)


def dot_nt(a, b):
    return lax.dot_general(a, b, (((1,), (1,)), ((), ())), preferred_element_type=F32)


def dot_tn(a, b):
    return lax.dot_general(a, b, (((0,), (0,)), ((), ())), preferred_element_type=F32)


def split_state(state):
    high = state.astype(BF16)
    return high, (state - high.astype(F32)).astype(BF16)


def times_state(a, state):
    high, low = split_state(state)
    return dot_nn(jnp.concatenate([a, a], axis=1), jnp.concatenate([high, low], axis=0))


def times_state_t(a, state):
    high, low = split_state(state)
    return dot_nt(jnp.concatenate([a, a], axis=1), jnp.concatenate([high, low], axis=1))


def masked(scores, lower):
    row = lax.broadcasted_iota(jnp.int32, scores.shape, 0)
    column = lax.broadcasted_iota(jnp.int32, scores.shape, 1)
    keep = (row >= column) if lower else (row <= column)
    return jnp.where(keep, scores, 0.0).astype(BF16)


def causal_product(a, b, values):
    top = masked(dot_nt(a[:HALF], b[:HALF]), True)
    left = dot_nt(a[HALF:], b[:HALF]).astype(BF16)
    right = masked(dot_nt(a[HALF:], b[HALF:]), True)
    first = dot_nn(top, values[:HALF])
    second = dot_nn(jnp.concatenate([left, right], axis=1), values)
    return first, second


def anticausal_product(a, b, values):
    left = masked(dot_nt(a[:HALF], b[:HALF]), False)
    right = dot_nt(a[:HALF], b[HALF:]).astype(BF16)
    bottom = masked(dot_nt(a[HALF:], b[HALF:]), False)
    first = dot_nn(jnp.concatenate([left, right], axis=1), values)
    second = dot_nn(bottom, values[HALF:])
    return first, second


WIDE = HEADS_HERE * DH
HALF_WIDE = OWNED * DH


def shape(dims, dtype=F32):
    return jax.ShapeDtypeStruct(dims, dtype)


def vmem():
    return pl.BlockSpec(memory_space=pltpu.VMEM)


def smem():
    return pl.BlockSpec(memory_space=pltpu.SMEM)


def hbm():
    return pl.BlockSpec(memory_space=pltpu.HBM)


def call(kernel, name, outs, core, *args, ins=None, out_places=None, scratch=(), limit=8 * MIB, aliases={}):
    ins = [vmem()] * len(args) if ins is None else ins
    out_places = [vmem()] * len(outs) if out_places is None else out_places
    return pl.pallas_call(
        kernel,
        in_specs=[smem()] + ins,
        out_specs=out_places,
        out_shape=outs,
        scratch_shapes=list(scratch),
        input_output_aliases=aliases,
        compiler_params=pltpu.CompilerParams(vmem_limit_bytes=limit),
        name=name,
    )(core, *args)


def head_columns(core, owned, index):
    first = OWNED * (core[0] if owned else 1 - core[0])
    return pl.ds(pl.multiple_of((first + index) * DH, DH), DH)


def local_columns(index):
    return slice(index * DH, (index + 1) * DH)


def turn_keys_kernel(core, column, keys, turned):
    for head in range(HEADS_HERE):
        columns = local_columns(head)
        turned[head] = keys[:, columns].T


def states_kernel(core, turned, values, theirs, mine):
    for owned, states in ((False, theirs), (True, mine)):
        for index in range(OWNED):
            head = OWNED * (core[0] if owned else 1 - core[0]) + index
            states[index] = dot_nn(turned[head], values[:, head_columns(core, owned, index)])


def intra_kernel(owned, core, queries, keys, values, intra, *done):
    for index in range(OWNED):
        columns, here = head_columns(core, owned, index), local_columns(index)
        first, second = causal_product(queries[:, columns], keys[:, columns], values[:, columns])
        intra[:HALF, here] = first
        intra[HALF:, here] = second
    for mark in done:
        mark[...] = jnp.zeros_like(mark)


def gates_kernel(core, gate, dout, gain, normed_own, normed_other, gain_here):
    for owned, normed in ((True, normed_own), (False, normed_other)):
        for index in range(OWNED):
            columns, here = head_columns(core, owned, index), local_columns(index)
            normed[:, here] = dout[:, columns].astype(F32) * jax.nn.sigmoid(gate[:, columns].astype(F32))
    gain_here[...] = gain[...]


def turned_kernel(owned, core, queries, keys, top, bottom, turned_query, done):
    for index in range(OWNED):
        columns = head_columns(core, owned, index)
        query, key = queries[:, columns], keys[:, columns]
        top[index, :, :HALF] = masked(dot_nt(key[:HALF], query[:HALF]), False)
        top[index, :, HALF:] = dot_nt(key[:HALF], query[HALF:]).astype(BF16)
        bottom[index] = masked(dot_nt(key[HALF:], query[HALF:]), False)
        turned_query[index] = query.T
    done[...] = jnp.zeros_like(done)


def attend_half(core, owned, queries, intra, normed, gain, state, attn_out):
    squares = products = None
    for index in range(OWNED):
        columns, here = head_columns(core, owned, index), local_columns(index)
        out = intra[:, here] + times_state(queries[:, columns], state[index, :DH])
        attn_out[:, here] = out
        square = out * out
        product = out * (normed[:, here] * gain[:, columns])
        squares = square if squares is None else squares + square
        products = product if products is None else products + product
    return squares, products


def attend_own_kernel(core, queries, intra, normed, gain, state, attn_out, squares, products):
    squares[...], products[...] = attend_half(core, True, queries, intra, normed, gain, state, attn_out)


def attend_other_kernel(core, queries, intra, normed, gain, state, squares, products, attn_out, sums):
    found = attend_half(core, False, queries, intra, normed, gain, state, attn_out)
    for which, (acc, more) in enumerate(zip((squares, products), found)):
        total = acc[...] + more
        for part in range(BLOCK // DH):
            turned = total[part * DH:(part + 1) * DH, :].T
            place = which * (BLOCK // DH) + part
            sums[place:place + 1, :] = jnp.sum(turned, axis=0, keepdims=True)


def grads_half(core, owned, turned_queries, attn_out, normed, gain, scale, cubes, grad, states):
    for index in range(OWNED):
        columns, here = head_columns(core, owned, index), local_columns(index)
        out, rate, one = attn_out[:, here], scale[...], normed[:, here]
        part = (rate * (one * gain[:, columns]) - out * cubes[...]).astype(BF16)
        grad[:, here] = part
        states[index, :DH] = dot_nn(turned_queries[index], part)
        row = jnp.sum(one * out * rate, axis=0, keepdims=True)
        states[index, DH:] = jnp.broadcast_to(row, (EXTRA, DH))


def add_kernel(core, one, other, *done_and_total):
    done_and_total[-1][...] = one[...] + other[...]


def grads_theirs_kernel(core, pair, other_pair, turned_done, early_done, turned_queries, attn_out, normed, gain,
                        grad, scale, cubes, theirs):
    whole = pair[...] + other_pair[...]
    for part in range(BLOCK // DH):
        rows = slice(part * DH, (part + 1) * DH)
        mean_square = whole[part:part + 1, :] / FEATURES
        mean_prod = whole[part + 4:part + 5, :] / FEATURES
        one = lax.rsqrt(mean_square + EPSILON)
        scale[rows, :] = jnp.broadcast_to(one, (DH, DH)).T
        cubes[rows, :] = jnp.broadcast_to(one * one * one * mean_prod, (DH, DH)).T
    grads_half(core, False, turned_queries, attn_out, normed, gain, scale, cubes, grad, theirs)


def grads_mine_kernel(core, scale, cubes, turned_queries, attn_out, normed, gain, grad, mine):
    grads_half(core, True, turned_queries, attn_out, normed, gain, scale, cubes, grad, mine)


def each_head(core, *halves):
    for owned in (True, False):
        for index in range(OWNED):
            place = index if owned else OWNED + index
            arrays = [pair[0] if owned else pair[1] for pair in halves]
            yield head_columns(core, owned, index), local_columns(index), place, index, arrays


def early_kernel(owned, core, gate, attn_out, normed, gain, output, dgate, done):
    for index in range(OWNED):
        columns, here = head_columns(core, owned, index), local_columns(index)
        sig = jax.nn.sigmoid(gate[:, columns].astype(F32))
        scaled = attn_out[:, here] * gain[:, columns]
        output[:, here] = scaled * sig
        dgate[:, here] = normed[:, here] * scaled * (1.0 - sig)
    done[...] = jnp.zeros_like(done)


def outputs_kernel(core, scale, output_own, output_other, dgate_own, dgate_other, output, dgate, done):
    for columns, here, _, _, (early_output, early_dgate) in each_head(
        core, (output_own, output_other), (dgate_own, dgate_other)
    ):
        rate = scale[...]
        output[:, columns] = (early_output[:, here] * rate).astype(BF16)
        dgate[:, columns] = (early_dgate[:, here] * rate).astype(BF16)
    done[...] = jnp.zeros_like(done)


def copy_out(source, target, sem):
    copy = pltpu.make_async_copy(source, target, sem)
    copy.start()
    return copy


def query_kernel(core, keys, values, grad_own, grad_other, own, other, output_here,
                 grad_query, left_own, left_other, right_own, right_other, output, done, sem):
    copy = copy_out(output_here, output, sem)
    for columns, here, _, index, (grads, states, left, right) in each_head(
        core, (grad_own, grad_other), (own, other), (left_own, left_other), (right_own, right_other)
    ):
        grad, value, key = grads[:, here], values[:, columns], keys[:, columns]
        inter = times_state_t(grad, states[index, :DH])
        top = masked(dot_nt(grad[:HALF], value[:HALF]), True)
        low = dot_nt(grad[HALF:], value[:HALF]).astype(BF16)
        corner = masked(dot_nt(grad[HALF:], value[HALF:]), True)
        left[index, :HALF] = top
        left[index, HALF:] = low
        right[index] = corner
        first = dot_nn(top, key[:HALF])
        second = dot_nn(jnp.concatenate([low, corner], axis=1), key)
        grad_query[:HALF, columns] = (first + inter[:HALF]).astype(BF16)
        grad_query[HALF:, columns] = (second + inter[HALF:]).astype(BF16)
    done[...] = jnp.zeros_like(done)
    copy.wait()


def key_kernel(core, queries, left_own, left_other, right_own, right_other, dgate_here,
               key_own, key_other, dgate, done, sem):
    copy = copy_out(dgate_here, dgate, sem)
    for columns, here, _, index, (left, right, part) in each_head(
        core, (left_own, left_other), (right_own, right_other), (key_own, key_other)
    ):
        query = queries[:, columns]
        part[:HALF, here] = dot_tn(left[index], query)
        part[HALF:, here] = dot_tn(right[index], query[HALF:])
    done[...] = jnp.zeros_like(done)
    copy.wait()


def value_kernel(core, grad_own, grad_other, top_own, top_other, bottom_own, bottom_other, query_here,
                 value_own, value_other, grad_query, done, sem):
    copy = copy_out(query_here, grad_query, sem)
    for _, here, _, index, (grads, top, bottom, part) in each_head(
        core, (grad_own, grad_other), (top_own, top_other), (bottom_own, bottom_other), (value_own, value_other)
    ):
        part[:HALF, here] = dot_nn(top[index], grads[:, here])
        part[HALF:, here] = dot_nn(bottom[index], grads[HALF:, here])
    done[...] = jnp.zeros_like(done)
    copy.wait()


def last_half(owned, core, keys, values, part_key, part_value, states, grad_key, grad_value, key_buf, value_buf, sems):
    copies = []
    for index in range(OWNED):
        columns, here = head_columns(core, owned, index), local_columns(index)
        state = states[index, :DH]
        key_buf[index] = (part_key[:, here] + times_state_t(values[:, columns], state)).astype(BF16)
        value_buf[index] = (part_value[:, here] + times_state(keys[:, columns], state)).astype(BF16)
        for which, (buffer, target) in enumerate(((key_buf, grad_key), (value_buf, grad_value))):
            copy = pltpu.make_async_copy(buffer.at[index], target.at[:, columns], sems.at[which, index])
            copy.start()
            copies.append(copy)
    for copy in copies:
        copy.wait()


def last_own_kernel(core, keys, values, part_key, part_value, states, grad_key, grad_value, *scratch):
    last_half(True, core, keys, values, part_key, part_value, states, grad_key, grad_value, *scratch)


def last_other_kernel(core, keys, values, part_key, part_value, own, other, key_before, value_before,
                      grad_key, grad_value, dgain, dgain_buf, dgain_sem, *scratch):
    for owned, states in ((True, own), (False, other)):
        for index in range(OWNED):
            row = OWNED * (core[0] if owned else 1 - core[0]) + index
            dgain_buf[pl.ds(row, 1), :] = states[index, DH:DH + 1]
    copy = pltpu.make_async_copy(dgain_buf, dgain, dgain_sem)
    copy.start()
    last_half(False, core, keys, values, part_key, part_value, other, grad_key, grad_value, *scratch)
    copy.wait()


def piece_rows(place, rows):
    return slice(place * rows, place * rows + PIECE)


def pack_kernel(rows, reverse, core, mine, received, *done_and_results):
    *_, pieces, kept = done_and_results
    ahead = core[0] == (1 if reverse else 0)
    for head in range(OWNED):
        kept[head] = jnp.where(ahead, mine[head, :DH], received[head, :DH])
    for head in range(OWNED):
        for part in range(DH // PIECE):
            source = slice(part * PIECE, (part + 1) * PIECE)
            place = head * (DH // PIECE) + part
            pieces[piece_rows(place, rows)] = mine[head, source] + received[head, source]
    if rows > PIECE:
        gains = [mine[head, DH:DH + 1] + received[head, DH:DH + 1] for head in range(OWNED)]
        for place in range(ROW):
            pieces[place * rows + PIECE:(place + 1) * rows] = jnp.concatenate(gains, axis=0)


def row_total_kernel(rows, core, pieces, total):
    whole = pieces[:rows]
    for chip in range(1, ROW):
        whole = whole + pieces[chip * rows:(chip + 1) * rows]
    total[...] = whole


def prefix_kernel(rows, reverse, column, pieces, neighbour, pair, other_pair, *done_and_results):
    *_, sums, gains = done_and_results
    odd, high = lax.rem(column[0], 2) == 1, column[0] >= 2
    take_one = jnp.logical_not(odd) if reverse else odd
    take_pair = jnp.logical_not(high) if reverse else high
    total = jnp.where(take_one, neighbour[:PIECE], 0.0) + jnp.where(take_pair, other_pair[:PIECE], 0.0)
    order = range(ROW - 1, -1, -1) if reverse else range(ROW)
    for chip in order:
        sums[piece_rows(chip, PIECE)] = total
        total = total + pieces[piece_rows(chip, rows)]
    if rows > PIECE:
        gains[:OWNED] = pair[PIECE:] + other_pair[PIECE:]


def chips_prefix_kernel(core, pieces, sums):
    chips = COLUMN * ROW
    height = OWNED * DH // chips
    total = jnp.zeros((height, DH), F32)
    for chip in range(chips):
        rows = slice(chip * height, (chip + 1) * height)
        sums[rows] = total
        total = total + pieces[rows]


def unpack_kernel(rows, reverse, core, back, kept, gains, own, send):
    ahead = core[0] == (1 if reverse else 0)
    for head in range(OWNED):
        for part in range(DH // PIECE):
            target = slice(part * PIECE, (part + 1) * PIECE)
            state = back[piece_rows(head * (DH // PIECE) + part, PIECE)]
            both = state + kept[head, target]
            own[head, target] = jnp.where(ahead, state, both)
            send[head, target] = jnp.where(ahead, both, state)
        if rows > PIECE:
            whole = jnp.broadcast_to(gains[head:head + 1], (EXTRA, DH))
            own[head, DH:] = whole
            send[head, DH:] = whole


def device(column, row, core):
    return (column * ROW + row) * 2 + core


def moved(to_column):
    return [
        (device(y, z, c), device(to_column(y), z, c))
        for y in range(COLUMN) for z in range(ROW) for c in range(2)
    ]


CORES = [(i, i ^ 1) for i in range(2 * COLUMN * ROW)]
ROWS = [[device(y, z, c) for z in range(ROW)] for y in range(COLUMN) for c in range(2)]


def sums_beyond(core, column, mine, theirs, reverse, beside_first, beside_second, before=()):
    rows = PIECE + (OWNED if mine.shape[1] > DH else 0)

    def exchange(pieces):
        high = pieces.shape[0]
        pieces = pieces.reshape(ROW, 1, high // ROW * DH)
        return lax.all_to_all(pieces, "seq", 0, 0, axis_index_groups=ROWS).reshape(high, DH)

    received = lax.ppermute(theirs, "seq", CORES)
    pieces, kept = call(
        functools.partial(pack_kernel, rows, reverse), "pack", [shape((ROW * rows, DH)), shape((OWNED, DH, DH))],
        core, mine, received, *before,
    )
    pieces = exchange(pieces)
    (total,) = call(functools.partial(row_total_kernel, rows), "row_total", [shape((rows, DH))], core, pieces)
    neighbour = lax.ppermute(total, "seq", moved(lambda y: y ^ 1))
    first = beside_first()
    (pair,) = call(add_kernel, "pair_total", [shape((rows, DH))], core, total, neighbour, first)
    other_pair = lax.ppermute(pair, "seq", moved(lambda y: COLUMN - 1 - y))
    second = beside_second()
    sums, gains = call(
        functools.partial(prefix_kernel, rows, reverse), "prefix", [shape((ROW * PIECE, DH)), shape((8, DH))],
        column, pieces, neighbour, pair, other_pair, *second,
    )
    own, send = call(
        functools.partial(unpack_kernel, rows, reverse), "unpack", [shape(mine.shape)] * 2,
        core, exchange(sums), kept, gains,
    )
    return own, lax.ppermute(send, "seq", CORES)


def sums_before(core, mine, theirs, before):
    chips = COLUMN * ROW
    groups = [[2 * i + one for i in range(chips)] for one in range(2)]
    flat = (OWNED * DH, DH)

    def exchange(pieces):
        pieces = pieces.reshape(chips, 1, OWNED * DH // chips * DH)
        return lax.all_to_all(pieces, "seq", 0, 0, axis_index_groups=groups).reshape(flat)

    received = lax.ppermute(theirs, "seq", CORES)
    pieces, kept = call(
        functools.partial(pack_kernel, PIECE, False), "pack", [shape(flat), shape((OWNED, DH, DH))],
        core, mine, received, before,
    )
    (sums,) = call(chips_prefix_kernel, "prefix", [shape(flat)], core, exchange(pieces))
    own, send = call(
        functools.partial(unpack_kernel, PIECE, False), "unpack", [shape(mine.shape)] * 2,
        core, exchange(sums), kept, before,
    )
    return own, lax.ppermute(send, "seq", CORES)


def body(queries, keys, values, gate, gain, dout):
    index = lax.axis_index("seq").astype(jnp.int32)
    core = lax.rem(index, 2).reshape(1)
    column = lax.div(index, 2 * ROW).reshape(1)
    gain_row = gain.reshape(1, WIDE)
    half = shape((BLOCK, HALF_WIDE))
    half_low = shape((BLOCK, HALF_WIDE), BF16)
    wide = shape((BLOCK, WIDE), BF16)
    tokens = shape((BLOCK, DH))
    with_gain = shape((OWNED, DH + EXTRA, DH))
    done = shape((8, DH))

    state = shape((OWNED, DH, DH))
    (turned_keys,) = call(
        turn_keys_kernel, "turn_keys", [shape((HEADS_HERE, DH, BLOCK), BF16)], core, column, keys,
        ins=[smem(), vmem()],
    )
    theirs, mine = call(states_kernel, "states", [state, state], core, turned_keys, values)

    normed_own, normed_other, gain_row = call(
        gates_kernel, "gates", [half, half, shape((1, WIDE))], core, gate, dout, gain_row,
    )
    intra_own, intra_done = call(
        functools.partial(intra_kernel, True), "intra_own", [half, done], core, queries, keys, values,
    )
    own, other = sums_before(core, mine, theirs, intra_done)
    (intra_other,) = call(
        functools.partial(intra_kernel, False), "intra_other", [half], core, queries, keys, values,
    )
    out_own, squares, products = call(
        attend_own_kernel, "attend_own", [half, tokens, tokens],
        core, queries, intra_own, normed_own, gain_row, own,
    )
    out_other, sums = call(
        attend_other_kernel, "attend_other", [half, done],
        core, queries, intra_other, normed_other, gain_row, other, squares, products,
    )

    turned = {}

    def turned_part(owned):
        name = "turned_own" if owned else "turned_other"
        *turned[owned], ended = call(
            functools.partial(turned_kernel, owned), name,
            [shape((OWNED, HALF, BLOCK), BF16), shape((OWNED, HALF, HALF), BF16),
             shape((OWNED, DH, BLOCK), BF16), done],
            core, queries, keys,
        )
        return ended

    early = {}

    def early_part(owned, attn_out, normed):
        name = "early_own" if owned else "early_other"
        *early[owned], ended = call(
            functools.partial(early_kernel, owned), name, [half, half, done],
            core, gate, attn_out, normed, gain_row,
        )
        return ended

    ring = lax.axis_size("head")
    neighbour = lax.ppermute(sums, "head", [(i, i ^ 1) for i in range(ring)])
    (pair,) = call(
        add_kernel, "pair_sums", [done],
        core, sums, neighbour, turned_part(True), early_part(True, out_own, normed_own),
    )
    other_pair = lax.ppermute(pair, "head", [(i, ring - 1 - i) for i in range(ring)])
    grad_other, scale, cubes, theirs = call(
        grads_theirs_kernel, "grads_theirs", [half_low, tokens, tokens, with_gain],
        core, pair, other_pair, turned_part(False), early_part(False, out_other, normed_other),
        turned[False][2], out_other, normed_other, gain_row,
    )
    grad_own, mine = call(
        grads_mine_kernel, "grads_mine", [half_low, with_gain],
        core, scale, cubes, turned[True][2], out_own, normed_own, gain_row,
    )
    output, dgate, outputs_done = call(
        outputs_kernel, "outputs", [wide, wide, done],
        core, scale, early[True][0], early[False][0], early[True][1], early[False][1],
    )

    results = {}

    one_copy = [pltpu.SemaphoreType.DMA]

    left, right = shape((OWNED, BLOCK, HALF), BF16), shape((OWNED, HALF, HALF), BF16)

    def query_part():
        *results["query"], ended = call(
            query_kernel, "grad_query", [wide, left, left, right, right, wide, done],
            core, keys, values, grad_own, grad_other, own, other, output,
            out_places=[vmem()] * 5 + [hbm(), vmem()],
            scratch=one_copy,
        )
        return ended

    def key_part():
        *results["key"], ended = call(
            key_kernel, "grad_key", [half, half, wide, done],
            core, queries, *results["query"][1:5], dgate,
            out_places=[vmem(), vmem(), hbm(), vmem()],
            scratch=one_copy,
        )
        return ended

    def value_part():
        *results["value"], ended = call(
            value_kernel, "grad_value", [half, half, wide, done],
            core, grad_own, grad_other, turned[True][0], turned[False][0], turned[True][1], turned[False][1],
            results["query"][0],
            out_places=[vmem(), vmem(), hbm(), vmem()],
            scratch=one_copy,
        )
        return ended

    later_own, later_other = sums_beyond(
        core, column, mine, theirs, True, query_part, lambda: (key_part(), value_part()), (outputs_done,)
    )
    output = results["query"][5]
    key_own, key_other, dgate = results["key"]
    value_own, value_other, grad_query = results["value"]
    buffer = pltpu.VMEM((OWNED, BLOCK, DH), BF16)
    scratch = [buffer, buffer, pltpu.SemaphoreType.DMA((2, OWNED))]
    grad_key, grad_value = call(
        last_own_kernel, "last_own", [wide, wide], core, keys, values, key_own, value_own, later_own,
        out_places=[hbm(), hbm()],
        scratch=scratch,
    )
    grad_key, grad_value, dgain = call(
        last_other_kernel, "last_other", [wide, wide, shape((HEADS_HERE, DH))],
        core, keys, values, key_other, value_other, later_own, later_other, grad_key, grad_value,
        ins=[vmem()] * 6 + [hbm()] * 2,
        out_places=[hbm()] * 3,
        scratch=[pltpu.VMEM((HEADS_HERE, DH), F32), pltpu.SemaphoreType.DMA] + scratch,
        aliases={7: 0, 8: 1},
    )
    return output, grad_query, grad_key, grad_value, dgate, dgain.reshape(WIDE)


def solution(mesh):
    wide = P("seq", "head")
    return jax.shard_map(
        body,
        mesh=mesh,
        in_specs=(wide, wide, wide, wide, P("head"), wide),
        out_specs=(wide, wide, wide, wide, wide, P("head")),
        check_vma=False,
    )
```

```python
import functools
import jax
import jax.numpy as jnp
from jax import lax
from jax.experimental import pallas as pl
from jax.experimental.pallas import tpu as pltpu
from jax.sharding import PartitionSpec as P

DH = 128
BLOCK = 512
HALF = BLOCK // 2
HEADS_HERE = 8
OWNED = HEADS_HERE // 2
FEATURES = 4096
COLUMN = 4
ROW = 8
PIECE = OWNED * DH // ROW
EXTRA = 8
EPSILON = 1e-06

F32 = jnp.float32
BF16 = jnp.bfloat16
MIB = 1024 * 1024


def dot_nn(a, b):
    return lax.dot_general(a, b, (((1,), (0,)), ((), ())), preferred_element_type=F32)


def dot_nt(a, b):
    return lax.dot_general(a, b, (((1,), (1,)), ((), ())), preferred_element_type=F32)


def dot_tn(a, b):
    return lax.dot_general(a, b, (((0,), (0,)), ((), ())), preferred_element_type=F32)


def split_state(state):
    high = state.astype(BF16)
    return high, (state - high.astype(F32)).astype(BF16)


def times_state(a, state):
    high, low = split_state(state)
    return dot_nn(jnp.concatenate([a, a], axis=1), jnp.concatenate([high, low], axis=0))


def times_state_t(a, state):
    high, low = split_state(state)
    return dot_nt(jnp.concatenate([a, a], axis=1), jnp.concatenate([high, low], axis=1))


def masked(scores, lower):
    row = lax.broadcasted_iota(jnp.int32, scores.shape, 0)
    column = lax.broadcasted_iota(jnp.int32, scores.shape, 1)
    keep = (row >= column) if lower else (row <= column)
    return jnp.where(keep, scores, 0.0).astype(BF16)


def causal_product(a, turned, values):
    top = masked(dot_nn(a[:HALF], turned[:, :HALF]), True)
    left = dot_nn(a[HALF:], turned[:, :HALF]).astype(BF16)
    right = masked(dot_nn(a[HALF:], turned[:, HALF:]), True)
    first = dot_nn(top, values[:HALF])
    second = dot_nn(jnp.concatenate([left, right], axis=1), values)
    return first, second


def anticausal_product(a, b, values):
    left = masked(dot_nt(a[:HALF], b[:HALF]), False)
    right = dot_nt(a[:HALF], b[HALF:]).astype(BF16)
    bottom = masked(dot_nt(a[HALF:], b[HALF:]), False)
    first = dot_nn(jnp.concatenate([left, right], axis=1), values)
    second = dot_nn(bottom, values[HALF:])
    return first, second


WIDE = HEADS_HERE * DH
HALF_WIDE = OWNED * DH


def shape(dims, dtype=F32):
    return jax.ShapeDtypeStruct(dims, dtype)


def vmem():
    return pl.BlockSpec(memory_space=pltpu.VMEM)


def smem():
    return pl.BlockSpec(memory_space=pltpu.SMEM)


def hbm():
    return pl.BlockSpec(memory_space=pltpu.HBM)


def call(kernel, name, outs, core, *args, ins=None, out_places=None, scratch=(), limit=8 * MIB):
    ins = [vmem()] * len(args) if ins is None else ins
    out_places = [vmem()] * len(outs) if out_places is None else out_places
    return pl.pallas_call(
        kernel,
        in_specs=[smem()] + ins,
        out_specs=out_places,
        out_shape=outs,
        scratch_shapes=list(scratch),
        compiler_params=pltpu.CompilerParams(vmem_limit_bytes=limit),
        name=name,
    )(core, *args)


def head_columns(core, owned, index):
    first = OWNED * (core[0] if owned else 1 - core[0])
    return pl.ds(pl.multiple_of((first + index) * DH, DH), DH)


def local_columns(index):
    return slice(index * DH, (index + 1) * DH)


def turn_keys_kernel(core, column, keys, turned):
    for head in range(HEADS_HERE):
        columns = local_columns(head)
        turned[head] = keys[:, columns].T


def states_kernel(core, turned, values, theirs, mine):
    for owned, states in ((False, theirs), (True, mine)):
        for index in range(OWNED):
            head = OWNED * (core[0] if owned else 1 - core[0]) + index
            states[index] = dot_nn(turned[head], values[:, head_columns(core, owned, index)])


def intra_kernel(owned, core, queries, turned_keys, values, intra, *done):
    for index in range(OWNED):
        head = OWNED * (core[0] if owned else 1 - core[0]) + index
        columns, here = head_columns(core, owned, index), local_columns(index)
        first, second = causal_product(queries[:, columns], turned_keys[head], values[:, columns])
        intra[:HALF, here] = first
        intra[HALF:, here] = second
    for mark in done:
        mark[...] = jnp.zeros_like(mark)


def gates_kernel(core, gate, dout, gain, normed_own, normed_other, gain_here):
    for owned, normed in ((True, normed_own), (False, normed_other)):
        for index in range(OWNED):
            columns, here = head_columns(core, owned, index), local_columns(index)
            normed[:, here] = dout[:, columns].astype(F32) * jax.nn.sigmoid(gate[:, columns].astype(F32))
    gain_here[...] = gain[...]


def turned_kernel(owned, core, queries, keys, top, bottom, turned_query, done):
    for index in range(OWNED):
        columns = head_columns(core, owned, index)
        query, key = queries[:, columns], keys[:, columns]
        top[index, :, :HALF] = masked(dot_nt(key[:HALF], query[:HALF]), False)
        top[index, :, HALF:] = dot_nt(key[:HALF], query[HALF:]).astype(BF16)
        bottom[index] = masked(dot_nt(key[HALF:], query[HALF:]), False)
        turned_query[index] = query.T
    done[...] = jnp.zeros_like(done)


def attend_half(core, owned, queries, intra, normed, gain, state, attn_out):
    squares = products = None
    for index in range(OWNED):
        columns, here = head_columns(core, owned, index), local_columns(index)
        out = intra[:, here] + times_state(queries[:, columns], state[index, :DH])
        attn_out[:, here] = out
        square = out * out
        product = out * (normed[:, here] * gain[:, columns])
        squares = square if squares is None else squares + square
        products = product if products is None else products + product
    return squares, products


def attend_own_kernel(core, queries, intra, normed, gain, state, attn_out, squares, products):
    squares[...], products[...] = attend_half(core, True, queries, intra, normed, gain, state, attn_out)


def attend_other_kernel(core, queries, intra, normed, gain, state, squares, products, attn_out, sums):
    found = attend_half(core, False, queries, intra, normed, gain, state, attn_out)
    for which, (acc, more) in enumerate(zip((squares, products), found)):
        total = acc[...] + more
        for part in range(BLOCK // DH):
            turned = total[part * DH:(part + 1) * DH, :].T
            place = which * (BLOCK // DH) + part
            sums[place:place + 1, :] = jnp.sum(turned, axis=0, keepdims=True)


def grads_half(core, owned, turned_queries, attn_out, normed, gain, scale, cubes, grad, states):
    for index in range(OWNED):
        columns, here = head_columns(core, owned, index), local_columns(index)
        out, rate, one = attn_out[:, here], scale[...], normed[:, here]
        part = (rate * (one * gain[:, columns]) - out * cubes[...]).astype(BF16)
        grad[:, here] = part
        states[index, :DH] = dot_nn(turned_queries[index], part)
        row = jnp.sum(one * out * rate, axis=0, keepdims=True)
        states[index, DH:] = jnp.broadcast_to(row, (EXTRA, DH))


def add_kernel(core, one, other, *done_and_total):
    done_and_total[-1][...] = one[...] + other[...]


def grads_theirs_kernel(core, pair, other_pair, turned_done, early_done, turned_queries, attn_out, normed, gain,
                        grad, scale, cubes, theirs):
    whole = pair[...] + other_pair[...]
    for part in range(BLOCK // DH):
        rows = slice(part * DH, (part + 1) * DH)
        mean_square = whole[part:part + 1, :] / FEATURES
        mean_prod = whole[part + 4:part + 5, :] / FEATURES
        one = lax.rsqrt(mean_square + EPSILON)
        scale[rows, :] = jnp.broadcast_to(one, (DH, DH)).T
        cubes[rows, :] = jnp.broadcast_to(one * one * one * mean_prod, (DH, DH)).T
    grads_half(core, False, turned_queries, attn_out, normed, gain, scale, cubes, grad, theirs)


def grads_mine_kernel(core, scale, cubes, turned_queries, attn_out, normed, gain, grad, mine):
    grads_half(core, True, turned_queries, attn_out, normed, gain, scale, cubes, grad, mine)


def each_head(core, *halves):
    for owned in (True, False):
        for index in range(OWNED):
            place = index if owned else OWNED + index
            arrays = [pair[0] if owned else pair[1] for pair in halves]
            yield head_columns(core, owned, index), local_columns(index), place, index, arrays


def early_kernel(owned, core, gate, attn_out, normed, gain, output, dgate, done):
    for index in range(OWNED):
        columns, here = head_columns(core, owned, index), local_columns(index)
        sig = jax.nn.sigmoid(gate[:, columns].astype(F32))
        scaled = attn_out[:, here] * gain[:, columns]
        output[:, here] = scaled * sig
        dgate[:, here] = normed[:, here] * scaled * (1.0 - sig)
    done[...] = jnp.zeros_like(done)


def outputs_kernel(core, scale, output_own, output_other, dgate_own, dgate_other, output, dgate, done):
    for columns, here, _, _, (early_output, early_dgate) in each_head(
        core, (output_own, output_other), (dgate_own, dgate_other)
    ):
        rate = scale[...]
        output[:, columns] = (early_output[:, here] * rate).astype(BF16)
        dgate[:, columns] = (early_dgate[:, here] * rate).astype(BF16)
    done[...] = jnp.zeros_like(done)


def copy_out(source, target, sem):
    copy = pltpu.make_async_copy(source, target, sem)
    copy.start()
    return copy


def query_kernel(core, keys, values, grad_own, grad_other, own, other, output_here,
                 grad_query, left_own, left_other, right_own, right_other, output, done, sem):
    copy = copy_out(output_here, output, sem)
    for columns, here, _, index, (grads, states, left, right) in each_head(
        core, (grad_own, grad_other), (own, other), (left_own, left_other), (right_own, right_other)
    ):
        grad, value, key = grads[:, here], values[:, columns], keys[:, columns]
        inter = times_state_t(grad, states[index, :DH])
        top = masked(dot_nt(grad[:HALF], value[:HALF]), True)
        low = dot_nt(grad[HALF:], value[:HALF]).astype(BF16)
        corner = masked(dot_nt(grad[HALF:], value[HALF:]), True)
        left[index, :HALF] = top
        left[index, HALF:] = low
        right[index] = corner
        first = dot_nn(top, key[:HALF])
        second = dot_nn(jnp.concatenate([low, corner], axis=1), key)
        grad_query[:HALF, columns] = (first + inter[:HALF]).astype(BF16)
        grad_query[HALF:, columns] = (second + inter[HALF:]).astype(BF16)
    done[...] = jnp.zeros_like(done)
    copy.wait()


def key_kernel(core, queries, left_own, left_other, right_own, right_other, dgate_here, query_here,
               key_own, key_other, dgate, grad_query, done, sems):
    copies = [copy_out(dgate_here, dgate, sems.at[0]), copy_out(query_here, grad_query, sems.at[1])]
    for columns, here, _, index, (left, right, part) in each_head(
        core, (left_own, left_other), (right_own, right_other), (key_own, key_other)
    ):
        query = queries[:, columns]
        part[:HALF, here] = dot_tn(left[index], query)
        part[HALF:, here] = dot_tn(right[index], query[HALF:])
    done[...] = jnp.zeros_like(done)
    for copy in copies:
        copy.wait()


def value_kernel(core, grad, top, bottom, part_value, *done):
    for index in range(OWNED):
        here = local_columns(index)
        part_value[:HALF, here] = dot_nn(top[index], grad[:, here])
        part_value[HALF:, here] = dot_nn(bottom[index], grad[HALF:, here])
    for mark in done:
        mark[...] = jnp.zeros_like(mark)


def last_own_kernel(core, keys, values, part_key, part_value, states, grad_key, grad_value):
    for index in range(OWNED):
        columns, here = head_columns(core, True, index), local_columns(index)
        state = states[index, :DH]
        grad_key[:, here] = (part_key[:, here] + times_state_t(values[:, columns], state)).astype(BF16)
        grad_value[:, here] = (part_value[:, here] + times_state(keys[:, columns], state)).astype(BF16)


def last_other_kernel(core, keys, values, part_key, part_value, own, other, key_before, value_before,
                      grad_key, grad_value, dgain, key_buf, value_buf, dgain_buf, sems, own_sems, dgain_sem):
    first = pl.ds(pl.multiple_of(core[0] * HALF_WIDE, HALF_WIDE), HALF_WIDE)
    copies = [
        copy_out(key_before, grad_key.at[:, first], own_sems.at[0]),
        copy_out(value_before, grad_value.at[:, first], own_sems.at[1]),
    ]
    for owned, states in ((True, own), (False, other)):
        for index in range(OWNED):
            row = OWNED * (core[0] if owned else 1 - core[0]) + index
            dgain_buf[pl.ds(row, 1), :] = states[index, DH:DH + 1]
    copies.append(copy_out(dgain_buf, dgain, dgain_sem))
    for index in range(OWNED):
        columns, here = head_columns(core, False, index), local_columns(index)
        state = other[index, :DH]
        key_buf[index] = (part_key[:, here] + times_state_t(values[:, columns], state)).astype(BF16)
        copies.append(copy_out(key_buf.at[index], grad_key.at[:, columns], sems.at[0, index]))
        value_buf[index] = (part_value[:, here] + times_state(keys[:, columns], state)).astype(BF16)
        copies.append(copy_out(value_buf.at[index], grad_value.at[:, columns], sems.at[1, index]))
    for copy in copies:
        copy.wait()


def piece_rows(place, rows):
    return slice(place * rows, place * rows + PIECE)


def pack_kernel(rows, reverse, core, mine, received, *done_and_results):
    *_, pieces, kept = done_and_results
    ahead = core[0] == (1 if reverse else 0)
    for head in range(OWNED):
        kept[head] = jnp.where(ahead, mine[head, :DH], received[head, :DH])
    for head in range(OWNED):
        for part in range(DH // PIECE):
            source = slice(part * PIECE, (part + 1) * PIECE)
            place = head * (DH // PIECE) + part
            pieces[piece_rows(place, rows)] = mine[head, source] + received[head, source]
    if rows > PIECE:
        gains = [mine[head, DH:DH + 1] + received[head, DH:DH + 1] for head in range(OWNED)]
        for place in range(ROW):
            pieces[place * rows + PIECE:(place + 1) * rows] = jnp.concatenate(gains, axis=0)


def row_total_kernel(rows, core, pieces, total):
    whole = pieces[:rows]
    for chip in range(1, ROW):
        whole = whole + pieces[chip * rows:(chip + 1) * rows]
    total[...] = whole


def prefix_kernel(rows, reverse, column, pieces, neighbour, pair, other_pair, *done_and_results):
    *_, sums, gains = done_and_results
    odd, high = lax.rem(column[0], 2) == 1, column[0] >= 2
    take_one = jnp.logical_not(odd) if reverse else odd
    take_pair = jnp.logical_not(high) if reverse else high
    total = jnp.where(take_one, neighbour[:PIECE], 0.0) + jnp.where(take_pair, other_pair[:PIECE], 0.0)
    order = range(ROW - 1, -1, -1) if reverse else range(ROW)
    for chip in order:
        sums[piece_rows(chip, PIECE)] = total
        total = total + pieces[piece_rows(chip, rows)]
    if rows > PIECE:
        gains[:OWNED] = pair[PIECE:] + other_pair[PIECE:]


def chips_prefix_kernel(core, pieces, sums):
    chips = COLUMN * ROW
    height = OWNED * DH // chips
    total = jnp.zeros((height, DH), F32)
    for chip in range(chips):
        rows = slice(chip * height, (chip + 1) * height)
        sums[rows] = total
        total = total + pieces[rows]


def unpack_kernel(rows, reverse, core, back, kept, gains, own, send):
    ahead = core[0] == (1 if reverse else 0)
    for head in range(OWNED):
        for part in range(DH // PIECE):
            target = slice(part * PIECE, (part + 1) * PIECE)
            state = back[piece_rows(head * (DH // PIECE) + part, PIECE)]
            both = state + kept[head, target]
            own[head, target] = jnp.where(ahead, state, both)
            send[head, target] = jnp.where(ahead, both, state)
        if rows > PIECE:
            whole = jnp.broadcast_to(gains[head:head + 1], (EXTRA, DH))
            own[head, DH:] = whole
            send[head, DH:] = whole


def device(column, row, core):
    return (column * ROW + row) * 2 + core


def moved(to_column):
    return [
        (device(y, z, c), device(to_column(y), z, c))
        for y in range(COLUMN) for z in range(ROW) for c in range(2)
    ]


CORES = [(i, i ^ 1) for i in range(2 * COLUMN * ROW)]
ROWS = [[device(y, z, c) for z in range(ROW)] for y in range(COLUMN) for c in range(2)]


def sums_beyond(core, column, mine, theirs, reverse, beside_first, beside_second, before=()):
    rows = PIECE + (OWNED if mine.shape[1] > DH else 0)

    def exchange(pieces):
        high = pieces.shape[0]
        pieces = pieces.reshape(ROW, 1, high // ROW * DH)
        return lax.all_to_all(pieces, "seq", 0, 0, axis_index_groups=ROWS).reshape(high, DH)

    received = lax.ppermute(theirs, "seq", CORES)
    pieces, kept = call(
        functools.partial(pack_kernel, rows, reverse), "pack", [shape((ROW * rows, DH)), shape((OWNED, DH, DH))],
        core, mine, received, *before,
    )
    pieces = exchange(pieces)
    (total,) = call(functools.partial(row_total_kernel, rows), "row_total", [shape((rows, DH))], core, pieces)
    neighbour = lax.ppermute(total, "seq", moved(lambda y: y ^ 1))
    first = beside_first()
    (pair,) = call(add_kernel, "pair_total", [shape((rows, DH))], core, total, neighbour, first)
    other_pair = lax.ppermute(pair, "seq", moved(lambda y: COLUMN - 1 - y))
    second = beside_second()
    sums, gains = call(
        functools.partial(prefix_kernel, rows, reverse), "prefix", [shape((ROW * PIECE, DH)), shape((8, DH))],
        column, pieces, neighbour, pair, other_pair, *second,
    )
    own, send = call(
        functools.partial(unpack_kernel, rows, reverse), "unpack", [shape(mine.shape)] * 2,
        core, exchange(sums), kept, gains,
    )
    return own, lax.ppermute(send, "seq", CORES)


def sums_before(core, mine, theirs, before):
    chips = COLUMN * ROW
    groups = [[2 * i + one for i in range(chips)] for one in range(2)]
    flat = (OWNED * DH, DH)

    def exchange(pieces):
        pieces = pieces.reshape(chips, 1, OWNED * DH // chips * DH)
        return lax.all_to_all(pieces, "seq", 0, 0, axis_index_groups=groups).reshape(flat)

    received = lax.ppermute(theirs, "seq", CORES)
    pieces, kept = call(
        functools.partial(pack_kernel, PIECE, False), "pack", [shape(flat), shape((OWNED, DH, DH))],
        core, mine, received, before,
    )
    (sums,) = call(chips_prefix_kernel, "prefix", [shape(flat)], core, exchange(pieces))
    own, send = call(
        functools.partial(unpack_kernel, PIECE, False), "unpack", [shape(mine.shape)] * 2,
        core, exchange(sums), kept, before,
    )
    return own, lax.ppermute(send, "seq", CORES)


def body(queries, keys, values, gate, gain, dout):
    index = lax.axis_index("seq").astype(jnp.int32)
    core = lax.rem(index, 2).reshape(1)
    column = lax.div(index, 2 * ROW).reshape(1)
    gain_row = gain.reshape(1, WIDE)
    half = shape((BLOCK, HALF_WIDE))
    half_low = shape((BLOCK, HALF_WIDE), BF16)
    wide = shape((BLOCK, WIDE), BF16)
    tokens = shape((BLOCK, DH))
    with_gain = shape((OWNED, DH + EXTRA, DH))
    done = shape((8, DH))

    state = shape((OWNED, DH, DH))
    (turned_keys,) = call(
        turn_keys_kernel, "turn_keys", [shape((HEADS_HERE, DH, BLOCK), BF16)], core, column, keys,
        ins=[smem(), vmem()],
    )
    theirs, mine = call(states_kernel, "states", [state, state], core, turned_keys, values)

    normed_own, normed_other, gain_row = call(
        gates_kernel, "gates", [half, half, shape((1, WIDE))], core, gate, dout, gain_row,
    )
    intra_own, intra_done = call(
        functools.partial(intra_kernel, True), "intra_own", [half, done], core, queries, turned_keys, values,
    )
    own, other = sums_before(core, mine, theirs, intra_done)
    (intra_other,) = call(
        functools.partial(intra_kernel, False), "intra_other", [half], core, queries, turned_keys, values,
    )
    out_own, squares, products = call(
        attend_own_kernel, "attend_own", [half, tokens, tokens],
        core, queries, intra_own, normed_own, gain_row, own,
    )
    out_other, sums = call(
        attend_other_kernel, "attend_other", [half, done],
        core, queries, intra_other, normed_other, gain_row, other, squares, products,
    )

    turned = {}

    def turned_part(owned):
        name = "turned_own" if owned else "turned_other"
        *turned[owned], ended = call(
            functools.partial(turned_kernel, owned), name,
            [shape((OWNED, HALF, BLOCK), BF16), shape((OWNED, HALF, HALF), BF16),
             shape((OWNED, DH, BLOCK), BF16), done],
            core, queries, keys,
        )
        return ended

    early = {}

    def early_part(owned, attn_out, normed):
        name = "early_own" if owned else "early_other"
        *early[owned], ended = call(
            functools.partial(early_kernel, owned), name, [half, half, done],
            core, gate, attn_out, normed, gain_row,
        )
        return ended

    ring = lax.axis_size("head")
    neighbour = lax.ppermute(sums, "head", [(i, i ^ 1) for i in range(ring)])
    (pair,) = call(
        add_kernel, "pair_sums", [done],
        core, sums, neighbour, turned_part(True), early_part(True, out_own, normed_own),
    )
    other_pair = lax.ppermute(pair, "head", [(i, ring - 1 - i) for i in range(ring)])
    grad_other, scale, cubes, theirs = call(
        grads_theirs_kernel, "grads_theirs", [half_low, tokens, tokens, with_gain],
        core, pair, other_pair, turned_part(False), early_part(False, out_other, normed_other),
        turned[False][2], out_other, normed_other, gain_row,
    )
    grad_own, mine = call(
        grads_mine_kernel, "grads_mine", [half_low, with_gain],
        core, scale, cubes, turned[True][2], out_own, normed_own, gain_row,
    )
    output, dgate, outputs_done = call(
        outputs_kernel, "outputs", [wide, wide, done],
        core, scale, early[True][0], early[False][0], early[True][1], early[False][1],
    )

    results = {}

    one_copy = [pltpu.SemaphoreType.DMA]

    left, right = shape((OWNED, BLOCK, HALF), BF16), shape((OWNED, HALF, HALF), BF16)

    def query_part():
        *results["query"], ended = call(
            query_kernel, "grad_query", [wide, left, left, right, right, wide, done],
            core, keys, values, grad_own, grad_other, own, other, output,
            out_places=[vmem()] * 5 + [hbm(), vmem()],
            scratch=one_copy,
        )
        return ended

    def key_part():
        *results["key"], ended = call(
            key_kernel, "grad_key", [half, half, wide, wide, done],
            core, queries, *results["query"][1:5], dgate, results["query"][0],
            out_places=[vmem(), vmem(), hbm(), hbm(), vmem()],
            scratch=[pltpu.SemaphoreType.DMA((2,))],
        )
        return ended

    def value_part():
        results["value"], ended = call(
            value_kernel, "value_own", [half, done], core, grad_own, *turned[True][:2],
        )
        return ended

    later_own, later_other = sums_beyond(
        core, column, mine, theirs, True, query_part, lambda: (key_part(), value_part()), (outputs_done,)
    )
    output = results["query"][5]
    key_own, key_other, dgate, grad_query = results["key"]
    value_own = results["value"]
    (value_other,) = call(value_kernel, "value_other", [half], core, grad_other, *turned[False][:2])
    key_before, value_before = call(
        last_own_kernel, "last_own", [half_low, half_low], core, keys, values, key_own, value_own, later_own,
    )
    buffer = pltpu.VMEM((OWNED, BLOCK, DH), BF16)
    grad_key, grad_value, dgain = call(
        last_other_kernel, "last_other", [wide, wide, shape((HEADS_HERE, DH))],
        core, keys, values, key_other, value_other, later_own, later_other, key_before, value_before,
        out_places=[hbm()] * 3,
        scratch=[
            buffer, buffer, pltpu.VMEM((HEADS_HERE, DH), F32),
            pltpu.SemaphoreType.DMA((2, OWNED)), pltpu.SemaphoreType.DMA((2,)), pltpu.SemaphoreType.DMA,
        ],
    )
    return output, grad_query, grad_key, grad_value, dgate, dgain.reshape(WIDE)


def solution(mesh):
    wide = P("seq", "head")
    return jax.shard_map(
        body,
        mesh=mesh,
        in_specs=(wide, wide, wide, wide, P("head"), wide),
        out_specs=(wide, wide, wide, wide, wide, P("head")),
        check_vma=False,
    )
```

```python
import functools
import jax
import jax.numpy as jnp
from jax import lax
from jax.experimental import pallas as pl
from jax.experimental.pallas import tpu as pltpu
from jax.sharding import PartitionSpec as P

DH = 128
BLOCK = 512
HALF = BLOCK // 2
HEADS_HERE = 8
OWNED = HEADS_HERE // 2
FEATURES = 4096
COLUMN = 4
ROW = 8
PIECE = OWNED * DH // ROW
EXTRA = 8
EPSILON = 1e-06

F32 = jnp.float32
BF16 = jnp.bfloat16
MIB = 1024 * 1024


def dot_nn(a, b):
    return lax.dot_general(a, b, (((1,), (0,)), ((), ())), preferred_element_type=F32)


def dot_nt(a, b):
    return lax.dot_general(a, b, (((1,), (1,)), ((), ())), preferred_element_type=F32)


def dot_tn(a, b):
    return lax.dot_general(a, b, (((0,), (0,)), ((), ())), preferred_element_type=F32)


def split_state(state):
    high = state.astype(BF16)
    return high, (state - high.astype(F32)).astype(BF16)


def times_state(a, state):
    high, low = split_state(state)
    return dot_nn(jnp.concatenate([a, a], axis=1), jnp.concatenate([high, low], axis=0))


def times_state_t(a, state):
    high, low = split_state(state)
    return dot_nt(jnp.concatenate([a, a], axis=1), jnp.concatenate([high, low], axis=1))


def masked(scores, lower):
    row = lax.broadcasted_iota(jnp.int32, scores.shape, 0)
    column = lax.broadcasted_iota(jnp.int32, scores.shape, 1)
    keep = (row >= column) if lower else (row <= column)
    return jnp.where(keep, scores, 0.0).astype(BF16)


def causal_product(a, turned, values):
    top = masked(dot_nn(a[:HALF], turned[:, :HALF]), True)
    left = dot_nn(a[HALF:], turned[:, :HALF]).astype(BF16)
    right = masked(dot_nn(a[HALF:], turned[:, HALF:]), True)
    first = dot_nn(top, values[:HALF])
    second = dot_nn(jnp.concatenate([left, right], axis=1), values)
    return first, second


def anticausal_product(a, b, values):
    left = masked(dot_nt(a[:HALF], b[:HALF]), False)
    right = dot_nt(a[:HALF], b[HALF:]).astype(BF16)
    bottom = masked(dot_nt(a[HALF:], b[HALF:]), False)
    first = dot_nn(jnp.concatenate([left, right], axis=1), values)
    second = dot_nn(bottom, values[HALF:])
    return first, second


WIDE = HEADS_HERE * DH
HALF_WIDE = OWNED * DH


def shape(dims, dtype=F32):
    return jax.ShapeDtypeStruct(dims, dtype)


def vmem():
    return pl.BlockSpec(memory_space=pltpu.VMEM)


def smem():
    return pl.BlockSpec(memory_space=pltpu.SMEM)


def hbm():
    return pl.BlockSpec(memory_space=pltpu.HBM)


def call(kernel, name, outs, core, *args, ins=None, out_places=None, scratch=(), limit=8 * MIB):
    ins = [vmem()] * len(args) if ins is None else ins
    out_places = [vmem()] * len(outs) if out_places is None else out_places
    return pl.pallas_call(
        kernel,
        in_specs=[smem()] + ins,
        out_specs=out_places,
        out_shape=outs,
        scratch_shapes=list(scratch),
        compiler_params=pltpu.CompilerParams(vmem_limit_bytes=limit),
        name=name,
    )(core, *args)


def head_columns(core, owned, index):
    first = OWNED * (core[0] if owned else 1 - core[0])
    return pl.ds(pl.multiple_of((first + index) * DH, DH), DH)


def local_columns(index):
    return slice(index * DH, (index + 1) * DH)


def turn_keys_kernel(core, column, keys, turned):
    for head in range(HEADS_HERE):
        columns = local_columns(head)
        turned[head] = keys[:, columns].T


def states_kernel(core, turned, values, theirs, mine):
    for owned, states in ((False, theirs), (True, mine)):
        for index in range(OWNED):
            head = OWNED * (core[0] if owned else 1 - core[0]) + index
            states[index] = dot_nn(turned[head], values[:, head_columns(core, owned, index)])


def intra_kernel(owned, core, queries, turned_keys, values, intra, *done):
    for index in range(OWNED):
        head = OWNED * (core[0] if owned else 1 - core[0]) + index
        columns, here = head_columns(core, owned, index), local_columns(index)
        first, second = causal_product(queries[:, columns], turned_keys[head], values[:, columns])
        intra[:HALF, here] = first
        intra[HALF:, here] = second
    for mark in done:
        mark[...] = jnp.zeros_like(mark)


def gates_kernel(core, gate, dout, gain, normed_own, normed_other, gain_here):
    for owned, normed in ((True, normed_own), (False, normed_other)):
        for index in range(OWNED):
            columns, here = head_columns(core, owned, index), local_columns(index)
            normed[:, here] = dout[:, columns].astype(F32) * jax.nn.sigmoid(gate[:, columns].astype(F32))
    gain_here[...] = gain[...]


def turned_kernel(owned, core, queries, keys, top, bottom, turned_query, done):
    for index in range(OWNED):
        columns = head_columns(core, owned, index)
        query, key = queries[:, columns], keys[:, columns]
        top[index, :, :HALF] = masked(dot_nt(key[:HALF], query[:HALF]), False)
        top[index, :, HALF:] = dot_nt(key[:HALF], query[HALF:]).astype(BF16)
        bottom[index] = masked(dot_nt(key[HALF:], query[HALF:]), False)
        turned_query[index] = query.T
    done[...] = jnp.zeros_like(done)


def attend_half(core, owned, queries, intra, normed, gain, state, attn_out):
    squares = products = None
    for index in range(OWNED):
        columns, here = head_columns(core, owned, index), local_columns(index)
        out = intra[:, here] + times_state(queries[:, columns], state[index, :DH])
        attn_out[:, here] = out
        square = out * out
        product = out * (normed[:, here] * gain[:, columns])
        squares = square if squares is None else squares + square
        products = product if products is None else products + product
    return squares, products


def attend_own_kernel(core, queries, intra, normed, gain, state, attn_out, squares, products):
    squares[...], products[...] = attend_half(core, True, queries, intra, normed, gain, state, attn_out)


def attend_other_kernel(core, queries, intra, normed, gain, state, squares, products, attn_out, sums):
    found = attend_half(core, False, queries, intra, normed, gain, state, attn_out)
    for which, (acc, more) in enumerate(zip((squares, products), found)):
        total = acc[...] + more
        for part in range(BLOCK // DH):
            turned = total[part * DH:(part + 1) * DH, :].T
            place = which * (BLOCK // DH) + part
            sums[place:place + 1, :] = jnp.sum(turned, axis=0, keepdims=True)


def grads_half(core, owned, turned_queries, attn_out, normed, gain, scale, cubes, grad, states):
    for index in range(OWNED):
        columns, here = head_columns(core, owned, index), local_columns(index)
        out, rate, one = attn_out[:, here], scale[...], normed[:, here]
        part = (rate * (one * gain[:, columns]) - out * cubes[...]).astype(BF16)
        grad[:, here] = part
        states[index, :DH] = dot_nn(turned_queries[index], part)
        row = jnp.sum(one * out * rate, axis=0, keepdims=True)
        states[index, DH:] = jnp.broadcast_to(row, (EXTRA, DH))


def add_kernel(core, one, other, *done_and_total):
    done_and_total[-1][...] = one[...] + other[...]


def grads_theirs_kernel(core, pair, other_pair, turned_done, early_done, turned_queries, attn_out, normed, gain,
                        grad, scale, cubes, theirs):
    whole = pair[...] + other_pair[...]
    for part in range(BLOCK // DH):
        rows = slice(part * DH, (part + 1) * DH)
        mean_square = whole[part:part + 1, :] / FEATURES
        mean_prod = whole[part + 4:part + 5, :] / FEATURES
        one = lax.rsqrt(mean_square + EPSILON)
        scale[rows, :] = jnp.broadcast_to(one, (DH, DH)).T
        cubes[rows, :] = jnp.broadcast_to(one * one * one * mean_prod, (DH, DH)).T
    grads_half(core, False, turned_queries, attn_out, normed, gain, scale, cubes, grad, theirs)


def grads_mine_kernel(core, scale, cubes, turned_queries, attn_out, normed, gain, grad, mine):
    grads_half(core, True, turned_queries, attn_out, normed, gain, scale, cubes, grad, mine)


def each_head(core, *halves):
    for owned in (True, False):
        for index in range(OWNED):
            place = index if owned else OWNED + index
            arrays = [pair[0] if owned else pair[1] for pair in halves]
            yield head_columns(core, owned, index), local_columns(index), place, index, arrays


def early_kernel(owned, core, gate, attn_out, normed, gain, output, dgate, done):
    for index in range(OWNED):
        columns, here = head_columns(core, owned, index), local_columns(index)
        sig = jax.nn.sigmoid(gate[:, columns].astype(F32))
        scaled = attn_out[:, here] * gain[:, columns]
        output[:, here] = scaled * sig
        dgate[:, here] = normed[:, here] * scaled * (1.0 - sig)
    done[...] = jnp.zeros_like(done)


def outputs_kernel(core, scale, output_own, output_other, dgate_own, dgate_other, output, dgate, done):
    for columns, here, _, _, (early_output, early_dgate) in each_head(
        core, (output_own, output_other), (dgate_own, dgate_other)
    ):
        rate = scale[...]
        output[:, columns] = (early_output[:, here] * rate).astype(BF16)
        dgate[:, columns] = (early_dgate[:, here] * rate).astype(BF16)
    done[...] = jnp.zeros_like(done)


def copy_out(source, target, sem):
    copy = pltpu.make_async_copy(source, target, sem)
    copy.start()
    return copy


def query_kernel(core, keys, values, grad_own, grad_other, own, other,
                 grad_query, left_own, left_other, right_own, right_other, done):
    for columns, here, _, index, (grads, states, left, right) in each_head(
        core, (grad_own, grad_other), (own, other), (left_own, left_other), (right_own, right_other)
    ):
        grad, value, key = grads[:, here], values[:, columns], keys[:, columns]
        inter = times_state_t(grad, states[index, :DH])
        top = masked(dot_nt(grad[:HALF], value[:HALF]), True)
        low = dot_nt(grad[HALF:], value[:HALF]).astype(BF16)
        corner = masked(dot_nt(grad[HALF:], value[HALF:]), True)
        left[index, :HALF] = top
        left[index, HALF:] = low
        right[index] = corner
        first = dot_nn(top, key[:HALF])
        second = dot_nn(jnp.concatenate([low, corner], axis=1), key)
        grad_query[:HALF, columns] = (first + inter[:HALF]).astype(BF16)
        grad_query[HALF:, columns] = (second + inter[HALF:]).astype(BF16)
    done[...] = jnp.zeros_like(done)


def key_kernel(core, queries, left_own, left_other, right_own, right_other, dgate_here, query_here,
               key_own, key_other, dgate, grad_query, done, sems):
    copies = [copy_out(dgate_here, dgate, sems.at[0]), copy_out(query_here, grad_query, sems.at[1])]
    for columns, here, _, index, (left, right, part) in each_head(
        core, (left_own, left_other), (right_own, right_other), (key_own, key_other)
    ):
        query = queries[:, columns]
        part[:HALF, here] = dot_tn(left[index], query)
        part[HALF:, here] = dot_tn(right[index], query[HALF:])
    done[...] = jnp.zeros_like(done)
    for copy in copies:
        copy.wait()


def value_kernel(core, grad, top, bottom, part_value, *done):
    for index in range(OWNED):
        here = local_columns(index)
        part_value[:HALF, here] = dot_nn(top[index], grad[:, here])
        part_value[HALF:, here] = dot_nn(bottom[index], grad[HALF:, here])
    for mark in done:
        mark[...] = jnp.zeros_like(mark)


def value_own_kernel(core, grad, top, bottom, output_here, part_value, output, done, sem):
    copy = copy_out(output_here, output, sem)
    value_kernel(core, grad, top, bottom, part_value, done)
    copy.wait()


def last_own_kernel(core, keys, values, part_key, part_value, states, grad_key, grad_value):
    for index in range(OWNED):
        columns, here = head_columns(core, True, index), local_columns(index)
        state = states[index, :DH]
        grad_key[:, here] = (part_key[:, here] + times_state_t(values[:, columns], state)).astype(BF16)
        grad_value[:, here] = (part_value[:, here] + times_state(keys[:, columns], state)).astype(BF16)


def last_other_kernel(core, keys, values, part_key, part_value, own, other, key_before, value_before,
                      grad_key, grad_value, dgain, key_buf, value_buf, dgain_buf, sems, own_sems, dgain_sem):
    first = pl.ds(pl.multiple_of(core[0] * HALF_WIDE, HALF_WIDE), HALF_WIDE)
    copies = [
        copy_out(key_before, grad_key.at[:, first], own_sems.at[0]),
        copy_out(value_before, grad_value.at[:, first], own_sems.at[1]),
    ]
    for owned, states in ((True, own), (False, other)):
        for index in range(OWNED):
            row = OWNED * (core[0] if owned else 1 - core[0]) + index
            dgain_buf[pl.ds(row, 1), :] = states[index, DH:DH + 1]
    copies.append(copy_out(dgain_buf, dgain, dgain_sem))
    for index in range(OWNED):
        columns, here = head_columns(core, False, index), local_columns(index)
        state = other[index, :DH]
        key_buf[index] = (part_key[:, here] + times_state_t(values[:, columns], state)).astype(BF16)
        copies.append(copy_out(key_buf.at[index], grad_key.at[:, columns], sems.at[0, index]))
        value_buf[index] = (part_value[:, here] + times_state(keys[:, columns], state)).astype(BF16)
        copies.append(copy_out(value_buf.at[index], grad_value.at[:, columns], sems.at[1, index]))
    for copy in copies:
        copy.wait()


def piece_rows(place, rows):
    return slice(place * rows, place * rows + PIECE)


def pack_kernel(rows, reverse, core, mine, received, *done_and_results):
    *_, pieces, kept = done_and_results
    ahead = core[0] == (1 if reverse else 0)
    for head in range(OWNED):
        kept[head] = jnp.where(ahead, mine[head, :DH], received[head, :DH])
    for head in range(OWNED):
        for part in range(DH // PIECE):
            source = slice(part * PIECE, (part + 1) * PIECE)
            place = head * (DH // PIECE) + part
            pieces[piece_rows(place, rows)] = mine[head, source] + received[head, source]
    if rows > PIECE:
        gains = [mine[head, DH:DH + 1] + received[head, DH:DH + 1] for head in range(OWNED)]
        for place in range(ROW):
            pieces[place * rows + PIECE:(place + 1) * rows] = jnp.concatenate(gains, axis=0)


def row_total_kernel(rows, core, pieces, total):
    whole = pieces[:rows]
    for chip in range(1, ROW):
        whole = whole + pieces[chip * rows:(chip + 1) * rows]
    total[...] = whole


def prefix_kernel(rows, reverse, column, pieces, neighbour, pair, other_pair, *done_and_results):
    *_, sums, gains = done_and_results
    odd, high = lax.rem(column[0], 2) == 1, column[0] >= 2
    take_one = jnp.logical_not(odd) if reverse else odd
    take_pair = jnp.logical_not(high) if reverse else high
    total = jnp.where(take_one, neighbour[:PIECE], 0.0) + jnp.where(take_pair, other_pair[:PIECE], 0.0)
    order = range(ROW - 1, -1, -1) if reverse else range(ROW)
    for chip in order:
        sums[piece_rows(chip, PIECE)] = total
        total = total + pieces[piece_rows(chip, rows)]
    if rows > PIECE:
        gains[:OWNED] = pair[PIECE:] + other_pair[PIECE:]


def chips_prefix_kernel(core, pieces, sums):
    chips = COLUMN * ROW
    height = OWNED * DH // chips
    total = jnp.zeros((height, DH), F32)
    for chip in range(chips):
        rows = slice(chip * height, (chip + 1) * height)
        sums[rows] = total
        total = total + pieces[rows]


def unpack_kernel(rows, reverse, core, back, kept, gains, own, send):
    ahead = core[0] == (1 if reverse else 0)
    for head in range(OWNED):
        for part in range(DH // PIECE):
            target = slice(part * PIECE, (part + 1) * PIECE)
            state = back[piece_rows(head * (DH // PIECE) + part, PIECE)]
            both = state + kept[head, target]
            own[head, target] = jnp.where(ahead, state, both)
            send[head, target] = jnp.where(ahead, both, state)
        if rows > PIECE:
            whole = jnp.broadcast_to(gains[head:head + 1], (EXTRA, DH))
            own[head, DH:] = whole
            send[head, DH:] = whole


def device(column, row, core):
    return (column * ROW + row) * 2 + core


def moved(to_column):
    return [
        (device(y, z, c), device(to_column(y), z, c))
        for y in range(COLUMN) for z in range(ROW) for c in range(2)
    ]


CORES = [(i, i ^ 1) for i in range(2 * COLUMN * ROW)]
ROWS = [[device(y, z, c) for z in range(ROW)] for y in range(COLUMN) for c in range(2)]


def sums_beyond(core, column, mine, theirs, reverse, beside_first, beside_second, before=()):
    rows = PIECE + (OWNED if mine.shape[1] > DH else 0)

    def exchange(pieces):
        high = pieces.shape[0]
        pieces = pieces.reshape(ROW, 1, high // ROW * DH)
        return lax.all_to_all(pieces, "seq", 0, 0, axis_index_groups=ROWS).reshape(high, DH)

    received = lax.ppermute(theirs, "seq", CORES)
    pieces, kept = call(
        functools.partial(pack_kernel, rows, reverse), "pack", [shape((ROW * rows, DH)), shape((OWNED, DH, DH))],
        core, mine, received, *before,
    )
    pieces = exchange(pieces)
    (total,) = call(functools.partial(row_total_kernel, rows), "row_total", [shape((rows, DH))], core, pieces)
    neighbour = lax.ppermute(total, "seq", moved(lambda y: y ^ 1))
    first = beside_first()
    (pair,) = call(add_kernel, "pair_total", [shape((rows, DH))], core, total, neighbour, first)
    other_pair = lax.ppermute(pair, "seq", moved(lambda y: COLUMN - 1 - y))
    second = beside_second()
    sums, gains = call(
        functools.partial(prefix_kernel, rows, reverse), "prefix", [shape((ROW * PIECE, DH)), shape((8, DH))],
        column, pieces, neighbour, pair, other_pair, *second,
    )
    own, send = call(
        functools.partial(unpack_kernel, rows, reverse), "unpack", [shape(mine.shape)] * 2,
        core, exchange(sums), kept, gains,
    )
    return own, lax.ppermute(send, "seq", CORES)


def sums_before(core, mine, theirs, before):
    chips = COLUMN * ROW
    groups = [[2 * i + one for i in range(chips)] for one in range(2)]
    flat = (OWNED * DH, DH)

    def exchange(pieces):
        pieces = pieces.reshape(chips, 1, OWNED * DH // chips * DH)
        return lax.all_to_all(pieces, "seq", 0, 0, axis_index_groups=groups).reshape(flat)

    received = lax.ppermute(theirs, "seq", CORES)
    pieces, kept = call(
        functools.partial(pack_kernel, PIECE, False), "pack", [shape(flat), shape((OWNED, DH, DH))],
        core, mine, received, before,
    )
    (sums,) = call(chips_prefix_kernel, "prefix", [shape(flat)], core, exchange(pieces))
    own, send = call(
        functools.partial(unpack_kernel, PIECE, False), "unpack", [shape(mine.shape)] * 2,
        core, exchange(sums), kept, before,
    )
    return own, lax.ppermute(send, "seq", CORES)


def body(queries, keys, values, gate, gain, dout):
    index = lax.axis_index("seq").astype(jnp.int32)
    core = lax.rem(index, 2).reshape(1)
    column = lax.div(index, 2 * ROW).reshape(1)
    gain_row = gain.reshape(1, WIDE)
    half = shape((BLOCK, HALF_WIDE))
    half_low = shape((BLOCK, HALF_WIDE), BF16)
    wide = shape((BLOCK, WIDE), BF16)
    tokens = shape((BLOCK, DH))
    with_gain = shape((OWNED, DH + EXTRA, DH))
    done = shape((8, DH))

    state = shape((OWNED, DH, DH))
    (turned_keys,) = call(
        turn_keys_kernel, "turn_keys", [shape((HEADS_HERE, DH, BLOCK), BF16)], core, column, keys,
        ins=[smem(), vmem()],
    )
    theirs, mine = call(states_kernel, "states", [state, state], core, turned_keys, values)

    normed_own, normed_other, gain_row = call(
        gates_kernel, "gates", [half, half, shape((1, WIDE))], core, gate, dout, gain_row,
    )
    intra_own, intra_done = call(
        functools.partial(intra_kernel, True), "intra_own", [half, done], core, queries, turned_keys, values,
    )
    own, other = sums_before(core, mine, theirs, intra_done)
    (intra_other,) = call(
        functools.partial(intra_kernel, False), "intra_other", [half], core, queries, turned_keys, values,
    )
    out_own, squares, products = call(
        attend_own_kernel, "attend_own", [half, tokens, tokens],
        core, queries, intra_own, normed_own, gain_row, own,
    )
    out_other, sums = call(
        attend_other_kernel, "attend_other", [half, done],
        core, queries, intra_other, normed_other, gain_row, other, squares, products,
    )

    turned = {}

    def turned_part(owned):
        name = "turned_own" if owned else "turned_other"
        *turned[owned], ended = call(
            functools.partial(turned_kernel, owned), name,
            [shape((OWNED, HALF, BLOCK), BF16), shape((OWNED, HALF, HALF), BF16),
             shape((OWNED, DH, BLOCK), BF16), done],
            core, queries, keys,
        )
        return ended

    early = {}

    def early_part(owned, attn_out, normed):
        name = "early_own" if owned else "early_other"
        *early[owned], ended = call(
            functools.partial(early_kernel, owned), name, [half, half, done],
            core, gate, attn_out, normed, gain_row,
        )
        return ended

    ring = lax.axis_size("head")
    neighbour = lax.ppermute(sums, "head", [(i, i ^ 1) for i in range(ring)])
    (pair,) = call(
        add_kernel, "pair_sums", [done],
        core, sums, neighbour, turned_part(True), early_part(True, out_own, normed_own),
    )
    other_pair = lax.ppermute(pair, "head", [(i, ring - 1 - i) for i in range(ring)])
    grad_other, scale, cubes, theirs = call(
        grads_theirs_kernel, "grads_theirs", [half_low, tokens, tokens, with_gain],
        core, pair, other_pair, turned_part(False), early_part(False, out_other, normed_other),
        turned[False][2], out_other, normed_other, gain_row,
    )
    grad_own, mine = call(
        grads_mine_kernel, "grads_mine", [half_low, with_gain],
        core, scale, cubes, turned[True][2], out_own, normed_own, gain_row,
    )
    output, dgate, outputs_done = call(
        outputs_kernel, "outputs", [wide, wide, done],
        core, scale, early[True][0], early[False][0], early[True][1], early[False][1],
    )

    results = {}

    one_copy = [pltpu.SemaphoreType.DMA]

    left, right = shape((OWNED, BLOCK, HALF), BF16), shape((OWNED, HALF, HALF), BF16)

    def query_part():
        *results["query"], ended = call(
            query_kernel, "grad_query", [wide, left, left, right, right, done],
            core, keys, values, grad_own, grad_other, own, other,
        )
        return ended

    def key_part():
        *results["key"], ended = call(
            key_kernel, "grad_key", [half, half, wide, wide, done],
            core, queries, *results["query"][1:5], dgate, results["query"][0],
            out_places=[vmem(), vmem(), hbm(), hbm(), vmem()],
            scratch=[pltpu.SemaphoreType.DMA((2,))],
        )
        return ended

    def value_part():
        *results["value"], ended = call(
            value_own_kernel, "value_own", [half, wide, done], core, grad_own, *turned[True][:2], output,
            out_places=[vmem(), hbm(), vmem()],
            scratch=one_copy,
        )
        return ended

    later_own, later_other = sums_beyond(
        core, column, mine, theirs, True, query_part, lambda: (key_part(), value_part()), (outputs_done,)
    )
    key_own, key_other, dgate, grad_query = results["key"]
    value_own, output_out = results["value"]
    (value_other,) = call(value_kernel, "value_other", [half], core, grad_other, *turned[False][:2])
    key_before, value_before = call(
        last_own_kernel, "last_own", [half_low, half_low], core, keys, values, key_own, value_own, later_own,
    )
    buffer = pltpu.VMEM((OWNED, BLOCK, DH), BF16)
    grad_key, grad_value, dgain = call(
        last_other_kernel, "last_other", [wide, wide, shape((HEADS_HERE, DH))],
        core, keys, values, key_other, value_other, later_own, later_other, key_before, value_before,
        out_places=[hbm()] * 3,
        scratch=[
            buffer, buffer, pltpu.VMEM((HEADS_HERE, DH), F32),
            pltpu.SemaphoreType.DMA((2, OWNED)), pltpu.SemaphoreType.DMA((2,)), pltpu.SemaphoreType.DMA,
        ],
    )
    return output_out, grad_query, grad_key, grad_value, dgate, dgain.reshape(WIDE)


def solution(mesh):
    wide = P("seq", "head")
    return jax.shard_map(
        body,
        mesh=mesh,
        in_specs=(wide, wide, wide, wide, P("head"), wide),
        out_specs=(wide, wide, wide, wide, wide, P("head")),
        check_vma=False,
    )
```
